32 devices in a mesh: cells: 8 (over z, y), spec: 4 (over x, core).
Axes of the slice: x: 2, y: 2, z: 4, core: 2. Of those that a mesh axis runs over, the one named last changes fastest.
Arguments:
- wind_field: float32 [2, 16, 16384], P(None, 'spec', 'cells'), may hold values from -6 to 6
- damping: float32 [16], P('spec'), may hold values from 0.002 to 0.02
- atm_table: int32 [3, 16384], P(None, 'cells'), may hold values from 0 to 3071, as said below
- atm_coef: float32 [3, 16384], P(None, 'cells'), may hold values from 0.5 to 1.5
- atm_send: int32 [8192], P('cells'), may hold values from 0 to 2047
- send_cells: int32 [64, 256], P('cells'), may hold values from 0 to 2047
- block_count: int32 [64], P('cells'), may hold values from 1 to 256, as said below
- slot_weight: float32 [64, 256], P('cells'), may hold values from 0.05 to 0.4
- recv_cells: int32 [64, 256], P('cells'), may hold values from 0 to 511
- spectra: float32 [36, 12, 4096], P(None, 'spec', 'cells'), may hold values from 0.005 to 16, as said below
- sea_mask: int32 [4096], P('cells'), may hold values 0 or 1
- ocn_table: int32 [3, 4096], P(None, 'cells'), may hold values from 0 to 767, as said below
- face_angle: float32 [3, 4096], P(None, 'cells'), may hold values from -3.140625 to 3.140625
- face_ratio: float32 [3, 4096], P(None, 'cells'), may hold values from 0.1 to 0.35
- ocn_send: int32 [2048], P('cells'), may hold values from 0 to 511
Outputs:
- wind_out: float32 [2, 16, 16384], P(None, 'spec', 'cells')
- spectra_new: float32 [36, 12, 4096], P(None, 'spec', 'cells')
The draws below stay inside these ranges and needn't reach their ends.
Inputs may be any that keep to these rules, and one draw needn't show every extreme that they name: `atm_table`: each own cell's entries point into its device's extended patch, within 512 positions of the cell's own place. `ocn_table`: each own cell's entries point into its device's extended patch, within 128 positions of the cell's own place. `block_count`: some ocean device receives 256 live slots from every atmosphere device. `spectra`: positive.
All inputs are finite; a program needn't handle non-finite values. No bound on the sum of `sea_mask` on one device may be relied on, other than what follows from the above.
Results may differ from the reference program's by a relative error of at most 0.00002.
Values sent between devices are 32-bit elements; how exact they have to be, the bound alone decides.
A program may use at most 64 MiB of HBM per device.

```python
import math
import jax
import jax.numpy as jnp
from jax import lax

ATM_CELLS = 2048
RIM_ATM = 512
OCN_CELLS = 512
RIM_OCN = 128
BLOCK_SLOTS = 256
DIRECTIONS = 36
BANDS = 12
LEVELS = 16
ATM_TOTAL = 16384
OCN_TOTAL = 4096
PAIRS = 64
N_CELLS = 8


def local_table(key, cells_dev, total, rim_width):
    offsets = jax.random.randint(key, (3, total), -rim_width, rim_width + 1, dtype=jnp.int32)
    local = jnp.arange(total, dtype=jnp.int32) % cells_dev
    table = local[None, :] + rim_width + offsets
    row_zero = jnp.arange(3, dtype=jnp.int32)[:, None] == 0
    table = jnp.where(row_zero & (local == 0)[None, :], 0, table)
    table = jnp.where(row_zero & (local == cells_dev - 1)[None, :], cells_dev + 2 * rim_width - 1, table)
    return table


def draw_atm_table(key, part):
    return local_table(jax.random.fold_in(key, 11), ATM_CELLS, ATM_TOTAL, RIM_ATM)


def draw_ocn_table(key, part):
    return local_table(jax.random.fold_in(key, 23), OCN_CELLS, OCN_TOTAL, RIM_OCN)


def draw_block_count(key, part):
    keys = jax.random.split(jax.random.fold_in(key, 37), 4)
    first = jax.random.randint(keys[0], (N_CELLS, N_CELLS), 0, BLOCK_SLOTS, dtype=jnp.int32)
    second = jax.random.randint(keys[1], (N_CELLS, N_CELLS), 0, BLOCK_SLOTS, dtype=jnp.int32)
    counts = 1 + first * second // BLOCK_SLOTS
    busiest = jax.random.randint(keys[2], (), 0, N_CELLS, dtype=jnp.int32)
    another = jax.random.randint(keys[3], (N_CELLS, 1), 0, N_CELLS, dtype=jnp.int32)
    column = jnp.arange(N_CELLS, dtype=jnp.int32)[None, :]
    counts = jnp.where((column == busiest) | (column == another), BLOCK_SLOTS, counts)
    return counts.reshape(-1)


def draw_spectra(key, part):
    keys = jax.random.split(jax.random.fold_in(key, 53), 2)
    shape = (DIRECTIONS, BANDS, OCN_TOTAL)
    position = jnp.arange(BANDS, dtype=jnp.float32) / (BANDS - 1)
    cell_scale = jnp.exp(jax.random.uniform(keys[1], (OCN_TOTAL,), jnp.float32, math.log(0.3), math.log(3.0)))
    base = jnp.exp(jax.random.uniform(keys[0], shape, jnp.float32, math.log(0.3), math.log(1.5)))
    profile = 3.0 ** position
    return base * profile[None, :, None] * cell_scale[None, None, :]


def set_ends(values, rng, least, top_value):
    spot = [jax.random.randint(jax.random.fold_in(rng, axis), (), 0, length) for axis, length in enumerate(values.shape)]
    longest = values.shape.index(max(values.shape))
    next_to = spot[:longest] + [(spot[longest] + 1) % values.shape[longest]] + spot[longest + 1:]
    return values.at[tuple(spot)].set(least).at[tuple(next_to)].set(top_value)


def level_of(own_key, shape, shards, low, top_value):
    def one(dim, blocks):
        heights = jax.random.uniform(jax.random.fold_in(jax.random.fold_in(own_key, 6), dim), (blocks,), jnp.float32, low / len(shards), top_value / len(shards))
        return jnp.repeat(jnp.exp(heights), shape[dim] // blocks).reshape((-1,) + (1,) * (len(shape) - dim - 1))

    loudness = one(*shards[0])
    for cut in shards[1:]:
        loudness = loudness * one(*cut)
    return loudness


def noise(key, shape, deviation, limit, shards=(), held_as=jnp.bfloat16):
    gain = level_of(key, shape, shards, -0.22, 0.18) if shards else 1.0
    drawn = jax.random.normal(key, shape, jnp.float32) * deviation * gain
    return jnp.minimum(jnp.maximum(drawn, -limit), limit).astype(held_as)


def setup_inputs(seed: int = 0) -> dict:
    splits = jax.random.split(jax.random.key(seed), 16)
    return {
        "wind_field": noise(splits[0], (2, LEVELS, ATM_TOTAL), 1.0, 6.0, ((1, 4), (2, 8)), jnp.float32),
        "damping": jnp.clip(jnp.exp(math.log(0.02) - 2.30258502 * jax.random.uniform(splits[1], (LEVELS,), jnp.float32) ** level_of(splits[1], (LEVELS,), ((0, 4),), -0.2, 0.2)), 0.002, 0.02),
        "atm_table": draw_atm_table(jax.random.fold_in(splits[15], 71), 0),
        "atm_coef": jnp.clip(jnp.exp(math.log(1.5) - 1.0986123 * jax.random.uniform(splits[3], (3, ATM_TOTAL), jnp.float32) ** level_of(splits[3], (3, ATM_TOTAL), ((1, 8),), -0.2, 0.2)), 0.5, 1.5),
        "atm_send": set_ends(jax.random.randint(splits[4], (2 * RIM_ATM * N_CELLS,), 0, ATM_CELLS), jax.random.fold_in(splits[4], 1), 0, ATM_CELLS - 1).astype(jnp.int32),
        "send_cells": set_ends(jax.random.randint(splits[5], (PAIRS, BLOCK_SLOTS), 0, ATM_CELLS), jax.random.fold_in(splits[5], 1), 0, ATM_CELLS - 1).astype(jnp.int32),
        "block_count": draw_block_count(jax.random.fold_in(splits[15], 71), 0),
        "slot_weight": jnp.clip(0.05 + 0.35 * jax.random.uniform(splits[7], (PAIRS, BLOCK_SLOTS), jnp.float32) ** level_of(splits[7], (PAIRS, BLOCK_SLOTS), ((0, 8),), -0.2, 0.2), 0.05, 0.4),
        "recv_cells": set_ends(jax.random.randint(splits[8], (PAIRS, BLOCK_SLOTS), 0, OCN_CELLS), jax.random.fold_in(splits[8], 1), 0, OCN_CELLS - 1).astype(jnp.int32),
        "spectra": draw_spectra(jax.random.fold_in(splits[15], 71), 0),
        "sea_mask": set_ends((jax.random.randint(splits[10], (OCN_TOTAL,), 0, 4) < 3).astype(jnp.int32), jax.random.fold_in(splits[10], 1), 0, 1),
        "ocn_table": draw_ocn_table(jax.random.fold_in(splits[15], 71), 0),
        "face_angle": jnp.clip(jax.random.uniform(splits[12], (3, OCN_TOTAL), jnp.float32, -3.140625, 3.140625), -3.140625, 3.140625),
        "face_ratio": jnp.clip(0.1 + 0.25 * jax.random.uniform(splits[13], (3, OCN_TOTAL), jnp.float32) ** level_of(splits[13], (3, OCN_TOTAL), ((1, 8),), -0.2, 0.2), 0.1, 0.35),
        "ocn_send": set_ends(jax.random.randint(splits[14], (2 * RIM_OCN * N_CELLS,), 0, OCN_CELLS), jax.random.fold_in(splits[14], 1), 0, OCN_CELLS - 1).astype(jnp.int32),
    }


epsilon = 1e-6
wind_factor = 0.8
growth = 0.1
coupling = 4.0
dissipation = 0.05


def laplace_cells(extended, fields, neighbours, lap_weight):
    gathered = extended[:, neighbours]
    return jnp.sum(lap_weight[None] * (gathered - fields[:, None, :]), axis=1)


def extend_all(fields, send_list, rim_width):
    packed = jax.vmap(lambda values, picks: values[:, picks], in_axes=(1, 0), out_axes=1)(fields, send_list)
    from_lower = jnp.roll(packed[:, :, rim_width:], 1, axis=1)
    from_upper = jnp.roll(packed[:, :, :rim_width], -1, axis=1)
    return jnp.concatenate([from_lower, fields, from_upper], axis=2)


def laplace_all(fields, send_list, neighbours, lap_weight, rim_width):
    extended = extend_all(fields, send_list, rim_width)
    return jax.vmap(laplace_cells, in_axes=(1, 1, 1, 1), out_axes=1)(extended, fields, neighbours, lap_weight)


def band_terms(energy, frequency):
    component_count = DIRECTIONS * BANDS
    mean_energy = jnp.sum(energy, axis=(0, 1)) / component_count
    inverse = jnp.sum(energy / frequency[None, :, None], axis=(0, 1)) / component_count
    return mean_energy, inverse


def sources(energy, wind, mean_energy, inverse, frequency, heading):
    wind_along = jnp.cos(heading)[:, None] * wind[0][None] + jnp.sin(heading)[:, None] * wind[1][None]
    gain_in = growth * frequency[None, :, None] * jnp.maximum(coupling * frequency[None, :, None] * wind_along[:, None, :] - 1.0, 0.0)
    mean_freq = mean_energy / (inverse + epsilon)
    decay_rate = dissipation * frequency[None, :, None] * (mean_energy * mean_freq ** 4)[None, None, :]
    return energy * (1.0 + gain_in) / (1.0 + decay_rate)


def propagate(energy, extended, neighbours, phase, ratio, group_speed, heading):
    result = energy
    for border in range(3):
        normal = jnp.cos(heading)[:, None] * jnp.cos(phase[border])[None] + jnp.sin(heading)[:, None] * jnp.sin(phase[border])[None]
        transport = group_speed[None, :, None] * normal[:, None, :] * ratio[border][None, None, :]
        upwind = extended[:, :, neighbours[border]]
        result = result - (jnp.maximum(transport, 0.0) * energy + jnp.minimum(transport, 0.0) * upwind)
    return result


def reference(wind_field, damping, atm_table, atm_coef, atm_send, send_cells, block_count, slot_weight, recv_cells, spectra, sea_mask, ocn_table, face_angle, face_ratio, ocn_send):
    fields = wind_field.reshape(2 * LEVELS, N_CELLS, ATM_CELLS)
    send_list = atm_send.reshape(N_CELLS, 2 * RIM_ATM)
    neighbours = atm_table.reshape(3, N_CELLS, ATM_CELLS)
    lap_weight = atm_coef.reshape(3, N_CELLS, ATM_CELLS)
    lap_once = laplace_all(fields, send_list, neighbours, lap_weight, RIM_ATM)
    lap_twice = laplace_all(lap_once, send_list, neighbours, lap_weight, RIM_ATM)
    damp_rate = jnp.concatenate([damping, damping])[:, None, None]
    damped = fields - damp_rate * lap_twice
    wind_out = damped.reshape(2, LEVELS, ATM_TOTAL)
    surface = wind_factor * damped.reshape(2, LEVELS, N_CELLS, ATM_CELLS)[:, LEVELS - 1]

    cell_slots = send_cells.reshape(N_CELLS, N_CELLS, BLOCK_SLOTS)
    counts = block_count.reshape(N_CELLS, N_CELLS)
    weights = slot_weight.reshape(N_CELLS, N_CELLS, BLOCK_SLOTS)
    active = jnp.arange(BLOCK_SLOTS, dtype=jnp.int32)[None, None, :] < counts[:, :, None]
    slot_scale = jnp.where(active, weights, 0.0)

    def pack(values, picks, scales):
        return values[:, picks] * scales[None]

    blocks = jax.vmap(pack, in_axes=(1, 0, 0), out_axes=1)(surface, cell_slots, slot_scale)
    arrive = jnp.transpose(blocks, (0, 2, 1, 3))
    targets = recv_cells.reshape(N_CELLS, N_CELLS, BLOCK_SLOTS)

    def deposit(values, places):
        return jnp.zeros((2, OCN_CELLS), jnp.float32).at[:, places.reshape(-1)].add(values.reshape(2, -1))

    ocean_wind = jax.vmap(deposit, in_axes=(1, 0), out_axes=1)(arrive, targets)

    frequency = 0.6 * 1.1 ** jnp.arange(BANDS, dtype=jnp.float32)
    group_speed = 0.5 / frequency
    heading = (jnp.arange(DIRECTIONS, dtype=jnp.float32) + 0.5) * (2.0 * math.pi / DIRECTIONS)
    energy = spectra.reshape(DIRECTIONS, BANDS, N_CELLS, OCN_CELLS) * sea_mask.reshape(N_CELLS, OCN_CELLS).astype(jnp.float32)[None, None]

    def source_cells(block_energy, wind):
        mean_energy, inverse = band_terms(block_energy, frequency)
        return sources(block_energy, wind, mean_energy, inverse, frequency, heading)

    updated = jax.vmap(source_cells, in_axes=(2, 1), out_axes=2)(energy, ocean_wind)
    flat = updated.reshape(DIRECTIONS * BANDS, N_CELLS, OCN_CELLS)
    extended = extend_all(flat, ocn_send.reshape(N_CELLS, 2 * RIM_OCN), RIM_OCN)
    extended = extended.reshape(DIRECTIONS, BANDS, N_CELLS, OCN_CELLS + 2 * RIM_OCN)
    members = (jnp.moveaxis(updated, 2, 0), jnp.moveaxis(extended, 2, 0),
               jnp.moveaxis(ocn_table.reshape(3, N_CELLS, OCN_CELLS), 1, 0),
               jnp.moveaxis(face_angle.reshape(3, N_CELLS, OCN_CELLS), 1, 0),
               jnp.moveaxis(face_ratio.reshape(3, N_CELLS, OCN_CELLS), 1, 0))
    result = lax.map(lambda member: propagate(member[0], member[1], member[2], member[3], member[4], group_speed, heading), members)
    spectra_new = jnp.moveaxis(result, 0, 2).reshape(DIRECTIONS, BANDS, OCN_TOTAL)
    return wind_out, spectra_new
```

```python
import functools
import math

import jax
import jax.numpy as jnp
from jax import lax
from jax.experimental import pallas as pl
from jax.experimental.pallas import tpu as pltpu
from jax.sharding import PartitionSpec as P

DIRECTIONS = 36
BANDS = 12
ROWS = 40
LANES = 128
MESH = pl.DeviceIdType.MESH

epsilon = 1e-06
wind_factor = 0.8
growth = 0.1
coupling = 4.0
dissipation = 0.05


def lane_take(tile, lane):
    return jnp.take_along_axis(tile, lane, axis=1, mode="promise_in_bounds")


def pick(tiles, lane, high, first):
    found = lane_take(tiles[0], lane)
    for j in range(1, len(tiles)):
        found = jnp.where(high == first + j, lane_take(tiles[j], lane), found)
    return found


def spread8(row):
    return jnp.broadcast_to(row, (8, row.shape[1]))


def split_index(index):
    return lax.bitwise_and(index, LANES - 1), lax.shift_right_logical(index, 7)


def kernel(
    n_cells, n_spec,
    wind, damping, atm_table, atm_coef, atm_send, send_cells, block_count, slot_weight, recv_cells,
    spectra, sea_mask, ocn_table, face_angle, face_ratio, ocn_send,
    wind_out, spectra_out,
    ext1, ext2, rim1, rim2, surf, blk_send, blk_recv, onehot, energy, means_own, means, inv_decay,
    trig, faces, ocn_rim, ocn_ext,
    atm_ssem, atm_rsem, mean_ssem, mean_rsem, surf_ssem, surf_rsem, blk_ssem, blk_rsem, ocn_ssem, ocn_rsem,
):
    me = lax.axis_index("cells")
    part = lax.axis_index("spec")
    before, after = lax.rem(me + n_cells - 1, n_cells), lax.rem(me + 1, n_cells)
    levels, cells = wind.shape[1], wind.shape[2]
    own_tiles = cells // LANES
    rim = rim1.shape[2]
    rim_tiles = rim // LANES
    bands, ocean = spectra.shape[1], spectra.shape[2]
    ocean_tiles = ocean // LANES
    slots = send_cells.shape[1]

    barrier = pltpu.get_barrier_semaphore()

    def greet_cells(step, carry):
        other = lax.rem(me + step, n_cells)
        pl.semaphore_signal(barrier, inc=1, device_id=(other, part), device_id_type=MESH)
        return carry

    def greet_spec(step, carry):
        other = lax.rem(part + step, n_spec)
        pl.semaphore_signal(barrier, inc=1, device_id=(me, other), device_id_type=MESH)
        return carry

    lax.fori_loop(1, n_cells, greet_cells, 0)
    lax.fori_loop(1, n_spec, greet_spec, 0)

    def gather_rim(ext, out):
        tiles = [ext[:, pl.ds(rim + j * LANES, LANES)] for j in range(own_tiles)]
        for t in range(2 * rim_tiles):
            lane, high = split_index(spread8(atm_send[pl.ds(t, 1), :]))
            out[t // rim_tiles, :, pl.ds((t % rim_tiles) * LANES, LANES)] = pick(tiles, lane, high, 0)

    def rim_copies(out, ext, base):
        to_before = pltpu.make_async_remote_copy(
            src_ref=out.at[0], dst_ref=ext.at[:, pl.ds(rim + cells, rim)],
            send_sem=atm_ssem.at[base], recv_sem=atm_rsem.at[base],
            device_id=(before, part), device_id_type=MESH)
        to_after = pltpu.make_async_remote_copy(
            src_ref=out.at[1], dst_ref=ext.at[:, pl.ds(0, rim)],
            send_sem=atm_ssem.at[base + 1], recv_sem=atm_rsem.at[base + 1],
            device_id=(after, part), device_id_type=MESH)
        return to_before, to_after

    def laplace(ext, store):
        def block(b, carry):
            start = pl.multiple_of(b * LANES, LANES)
            here = ext[:, pl.ds(rim + start, LANES)]
            tiles = [ext[:, pl.ds(start + j * LANES, LANES)] for j in range(2 * rim_tiles + 1)]
            total = jnp.zeros((8, LANES), jnp.float32)
            for k in range(3):
                lane, high = split_index(spread8(atm_table[pl.ds(k, 1), pl.ds(start, LANES)]))
                near = pick(tiles, lane, high - b, 0)
                total += spread8(atm_coef[pl.ds(k, 1), pl.ds(start, LANES)]) * (near - here)
            store(start, here, total)
            return carry

        lax.fori_loop(0, own_tiles, block, 0, unroll=4)

    ext1[0:levels, pl.ds(rim, cells)] = wind[0]
    ext1[levels:2 * levels, pl.ds(rim, cells)] = wind[1]
    gather_rim(ext1, rim1)
    pl.semaphore_wait(barrier, n_cells + n_spec - 2)
    first = rim_copies(rim1, ext1, 0)
    for copy in first:
        copy.start()

    mask = sea_mask[...].astype(jnp.float32)
    frequency = []
    for k in range(bands):
        value = jnp.float32(0.6 * 1.1**k)
        for s in range(1, n_spec):
            value = jnp.where(part == s, jnp.float32(0.6 * 1.1 ** (s * bands + k)), value)
        frequency.append(value)
    total = jnp.zeros((1, ocean), jnp.float32)
    inverse = jnp.zeros((1, ocean), jnp.float32)
    for k in range(bands):
        energy[k * ROWS + 32:(k + 1) * ROWS, :] = jnp.zeros((8, ocean), jnp.float32)
        band = spectra[:, k, :] * mask
        energy[k * ROWS:k * ROWS + DIRECTIONS, :] = band
        band_sum = jnp.sum(band, axis=0, keepdims=True)
        total += band_sum
        inverse += band_sum * (1.0 / jnp.full((1, ocean), frequency[k], jnp.float32))
    means_own[0:1, :] = total
    means_own[1:2, :] = inverse

    def mean_copy(other, slot):
        return pltpu.make_async_remote_copy(
            src_ref=means_own, dst_ref=means.at[slot],
            send_sem=mean_ssem.at[other], recv_sem=mean_rsem.at[slot],
            device_id=(me, other), device_id_type=MESH)

    for step in range(1, n_spec):
        mean_copy(lax.rem(part + step, n_spec), part).start()

    for copy in first:
        copy.wait_recv()

    def keep_once(start, here, lap):
        ext2[:, pl.ds(rim + start, LANES)] = lap

    laplace(ext1, keep_once)
    gather_rim(ext2, rim2)
    second = rim_copies(rim2, ext2, 2)
    for copy in second:
        copy.start()

    def mark(i, carry):
        place = lax.broadcasted_iota(jnp.int32, (ocean, slots), 0)
        hit = place == recv_cells[pl.ds(i, 1), :]
        onehot[:, pl.ds(pl.multiple_of(i * slots, LANES), slots)] = jnp.where(hit, 1.0, 0.0).astype(jnp.bfloat16)
        return carry

    lax.fori_loop(0, n_cells, mark, 0)
    heading = (lax.broadcasted_iota(jnp.int32, (ROWS, LANES), 0).astype(jnp.float32) + 0.5) * (
        2.0 * math.pi / DIRECTIONS
    )
    trig[0] = jnp.cos(heading)
    trig[1] = jnp.sin(heading)
    angle = face_angle[...]
    ratio = face_ratio[...]
    faces[0] = jnp.cos(angle) * ratio
    faces[1] = jnp.sin(angle) * ratio
    total = means_own[0:1, :]
    inverse = means_own[1:2, :]
    for step in range(1, n_spec):
        other = lax.rem(part + step, n_spec)
        mean_copy(other, other).wait_recv()
        total += means[other, 0:1, :]
        inverse += means[other, 1:2, :]
    count = DIRECTIONS * BANDS
    mean_energy = total / count
    mean_freq = mean_energy / (inverse / count + epsilon)
    squared = mean_freq * mean_freq
    for k in range(bands):
        decay = (dissipation * frequency[k]) * (mean_energy * (squared * squared))
        inv_decay[k:k + 1, :] = 1.0 / (1.0 + decay)

    for copy in second:
        copy.wait_recv()
    row = lax.broadcasted_iota(jnp.int32, (8, LANES), 0)
    rate = jnp.zeros((8, LANES), jnp.float32)
    for v in range(levels):
        rate = jnp.where(lax.rem(row, levels) == v, damping[v], rate)

    def keep_damped(start, here, lap):
        damped = ext1[:, pl.ds(rim + start, LANES)] - rate * lap
        wind_out[0, :, pl.ds(start, LANES)] = damped[0:levels]
        wind_out[1, :, pl.ds(start, LANES)] = damped[levels:2 * levels]

    laplace(ext2, keep_damped)

    def surf_copy(other):
        return pltpu.make_async_remote_copy(
            src_ref=surf, dst_ref=surf, send_sem=surf_ssem.at[other], recv_sem=surf_rsem,
            device_id=(me, other), device_id_type=MESH)

    @pl.when(part == n_spec - 1)
    def _():
        surf[0:1, :] = wind_factor * wind_out[0, levels - 1:levels, :]
        surf[1:2, :] = wind_factor * wind_out[1, levels - 1:levels, :]
        for other in range(n_spec - 1):
            surf_copy(other).start()

    @pl.when(part != n_spec - 1)
    def _():
        surf_copy(0).wait_recv()

    for g in range(n_cells // 8):
        row = lax.broadcasted_iota(jnp.int32, (8, LANES), 0)
        live = jnp.zeros((8, LANES), jnp.int32)
        for i in range(8):
            live = jnp.where(row == i, block_count[g * 8 + i], live)
        for h in range(slots // LANES):
            spot = lax.broadcasted_iota(jnp.int32, (8, LANES), 1) + h * LANES
            scale = jnp.where(spot < live, slot_weight[g * 8:g * 8 + 8, pl.ds(h * LANES, LANES)], 0.0)
            lane, high = split_index(send_cells[g * 8:g * 8 + 8, pl.ds(h * LANES, LANES)])
            for c in range(2):
                tiles = [spread8(surf[c:c + 1, pl.ds(j * LANES, LANES)]) for j in range(own_tiles)]
                blk_send[g * 8:g * 8 + 8, c, pl.ds(h * LANES, LANES)] = scale * pick(tiles, lane, high, 0)

    def block_copy(other, slot):
        return pltpu.make_async_remote_copy(
            src_ref=blk_send.at[other], dst_ref=blk_recv.at[slot],
            send_sem=blk_ssem.at[other], recv_sem=blk_rsem.at[slot],
            device_id=(other, part), device_id_type=MESH)

    def send_block(step, carry):
        block_copy(lax.rem(me + step, n_cells), me).start()
        return carry

    lax.fori_loop(1, n_cells, send_block, 0)
    blk_recv[me] = blk_send[me]

    def wait_block(step, carry):
        other = lax.rem(me + step, n_cells)
        block_copy(other, other).wait_recv()
        return carry

    lax.fori_loop(1, n_cells, wait_block, 0)

    def deposit(i, acc):
        value = blk_recv[i]
        high = value.astype(jnp.bfloat16).astype(jnp.float32)
        rest = value - high
        middle = rest.astype(jnp.bfloat16).astype(jnp.float32)
        parts = jnp.concatenate([high, middle, rest - middle, jnp.zeros_like(high)], axis=0)
        return acc + lax.dot_general(
            parts.astype(jnp.bfloat16), onehot[:, pl.ds(pl.multiple_of(i * slots, LANES), slots)],
            (((1,), (1,)), ((), ())), preferred_element_type=jnp.float32)

    acc = lax.fori_loop(0, n_cells, deposit, jnp.zeros((8, ocean), jnp.float32), unroll=8)
    wind_u = acc[0:1] + acc[2:3] + acc[4:5]
    wind_v = acc[1:2] + acc[3:4] + acc[5:6]

    for g in range(ROWS // 8):
        rows = slice(g * 8, g * 8 + 8)
        for b in range(ocean_tiles):
            at = slice(b * LANES, (b + 1) * LANES)
            along = trig[0, rows, :] * wind_u[:, at] + trig[1, rows, :] * wind_v[:, at]
            for k in range(bands):
                gain = (growth * frequency[k]) * jnp.maximum((coupling * frequency[k]) * along - 1.0, 0.0)
                spot = slice(k * ROWS + g * 8, k * ROWS + g * 8 + 8)
                ocn_ext[spot, LANES + b * LANES:LANES + (b + 1) * LANES] = (
                    energy[spot, at] * (1.0 + gain) * inv_decay[k:k + 1, at]
                )
    for side in range(2):
        lane, high = split_index(spread8(ocn_send[side:side + 1, :]))
        for r in range(bands * ROWS // 8):
            rows = slice(r * 8, r * 8 + 8)
            tiles = [ocn_ext[rows, LANES + j * LANES:LANES + (j + 1) * LANES] for j in range(ocean_tiles)]
            ocn_rim[side, rows, :] = pick(tiles, lane, high, 0)
    last = ocean + LANES
    third = (
        pltpu.make_async_remote_copy(
            src_ref=ocn_rim.at[0], dst_ref=ocn_ext.at[:, pl.ds(last, LANES)],
            send_sem=ocn_ssem.at[0], recv_sem=ocn_rsem.at[0],
            device_id=(before, part), device_id_type=MESH),
        pltpu.make_async_remote_copy(
            src_ref=ocn_rim.at[1], dst_ref=ocn_ext.at[:, pl.ds(0, LANES)],
            send_sem=ocn_ssem.at[1], recv_sem=ocn_rsem.at[1],
            device_id=(after, part), device_id_type=MESH),
    )
    for copy in third:
        copy.start()
    for copy in third:
        copy.wait_recv()

    for b in range(ocean_tiles):
        at = slice(b * LANES, (b + 1) * LANES)
        index = [split_index(spread8(ocn_table[f:f + 1, at])) for f in range(3)]
        for g in range(ROWS // 8):
            normal = [
                trig[0, g * 8:g * 8 + 8, :] * faces[0, f:f + 1, at] + trig[1, g * 8:g * 8 + 8, :] * faces[1, f:f + 1, at]
                for f in range(3)
            ]
            for k in range(bands):
                speed = 0.5 / jnp.full((8, LANES), frequency[k], jnp.float32)
                rows = slice(k * ROWS + g * 8, k * ROWS + g * 8 + 8)
                tiles = [ocn_ext[rows, (b + j) * LANES:(b + j + 1) * LANES] for j in range(3)]
                here = tiles[1]
                result = here
                for f in range(3):
                    transport = speed * normal[f]
                    upwind = pick(tiles, index[f][0], index[f][1], b)
                    result = result - transport * jnp.where(transport > 0.0, here, upwind)
                energy[rows, at] = result
    for k in range(bands):
        spectra_out[:, k, :] = energy[k * ROWS:k * ROWS + DIRECTIONS, :]

    for copy in (*first, *second, *third):
        copy.wait_send()
    for step in range(1, n_spec):
        mean_copy(lax.rem(part + step, n_spec), part).wait_send()

    @pl.when(part == n_spec - 1)
    def _():
        for other in range(n_spec - 1):
            surf_copy(other).wait_send()

    def sent_block(step, carry):
        block_copy(lax.rem(me + step, n_cells), me).wait_send()
        return carry

    lax.fori_loop(1, n_cells, sent_block, 0)


def local(
    n_cells, n_spec,
    wind_field, damping, atm_table, atm_coef, atm_send, send_cells, block_count, slot_weight, recv_cells,
    spectra, sea_mask, ocn_table, face_angle, face_ratio, ocn_send,
):
    levels, cells = wind_field.shape[1:]
    rim = atm_send.shape[0] // 2
    bands, ocean = spectra.shape[1:]
    slots = send_cells.shape[1]
    f32 = jnp.float32
    vmem = pl.BlockSpec(memory_space=pltpu.VMEM)
    smem = pl.BlockSpec(memory_space=pltpu.SMEM)
    dma = pltpu.SemaphoreType.DMA
    return pl.pallas_call(
        functools.partial(kernel, n_cells, n_spec),
        out_shape=(
            jax.ShapeDtypeStruct(wind_field.shape, f32),
            jax.ShapeDtypeStruct(spectra.shape, f32),
        ),
        in_specs=[vmem, smem, vmem, vmem, vmem, vmem, smem, vmem, vmem, vmem, vmem, vmem, vmem, vmem, vmem],
        out_specs=(vmem, vmem),
        scratch_shapes=[
            pltpu.VMEM((2 * levels, cells + 2 * rim), f32),
            pltpu.VMEM((2 * levels, cells + 2 * rim), f32),
            pltpu.VMEM((2, 2 * levels, rim), f32),
            pltpu.VMEM((2, 2 * levels, rim), f32),
            pltpu.VMEM((2, cells), f32),
            pltpu.VMEM((n_cells, 2, slots), f32),
            pltpu.VMEM((n_cells, 2, slots), f32),
            pltpu.VMEM((ocean, n_cells * slots), jnp.bfloat16),
            pltpu.VMEM((bands * ROWS, ocean), f32),
            pltpu.VMEM((2, ocean), f32),
            pltpu.VMEM((n_spec, 2, ocean), f32),
            pltpu.VMEM((bands, ocean), f32),
            pltpu.VMEM((2, ROWS, LANES), f32),
            pltpu.VMEM((2, 3, ocean), f32),
            pltpu.VMEM((2, bands * ROWS, LANES), f32),
            pltpu.VMEM((bands * ROWS, ocean + 2 * LANES), f32),
            dma((4,)), dma((4,)), dma((n_spec,)), dma((n_spec,)), dma((n_spec,)), dma,
            dma((n_cells,)), dma((n_cells,)), dma((2,)), dma((2,)),
        ],
        compiler_params=pltpu.CompilerParams(
            collective_id=0, has_side_effects=True, vmem_limit_bytes=(8 if n_cells <= 16 else 48) * 2**20
        ),
    )(
        wind_field, damping, atm_table, atm_coef, atm_send.reshape(-1, LANES), send_cells, block_count,
        slot_weight, recv_cells, spectra, sea_mask.reshape(1, -1), ocn_table, face_angle, face_ratio,
        ocn_send.reshape(-1, LANES),
    )


def solution(mesh):
    in_specs = (
        P(None, "spec", "cells"),
        P("spec"),
        P(None, "cells"),
        P(None, "cells"),
        P("cells"),
        P("cells", None),
        P("cells"),
        P("cells", None),
        P("cells", None),
        P(None, "spec", "cells"),
        P("cells"),
        P(None, "cells"),
        P(None, "cells"),
        P(None, "cells"),
        P("cells"),
    )
    out_specs = (P(None, "spec", "cells"), P(None, "spec", "cells"))
    body = functools.partial(local, mesh.shape["cells"], mesh.shape["spec"])
    return jax.shard_map(body, mesh=mesh, in_specs=in_specs, out_specs=out_specs, check_vma=False)
```

```python
import functools
import math

import jax
import jax.numpy as jnp
from jax import lax
from jax.experimental import pallas as pl
from jax.experimental.pallas import tpu as pltpu
from jax.sharding import PartitionSpec as P

DIRECTIONS = 36
BANDS = 12
ROWS = 40
LANES = 128
MESH = pl.DeviceIdType.MESH
LOADED = (
    "wind", "atm_send", "spectra", "sea_mask", "atm_table", "atm_coef", "recv_cells", "ocn_send", "face_angle",
    "face_ratio", "slot_weight", "send_cells", "ocn_table",
)

epsilon = 1e-06
wind_factor = 0.8
growth = 0.1
coupling = 4.0
dissipation = 0.05


def lane_take(tile, lane):
    return jnp.take_along_axis(tile, lane, axis=1, mode="promise_in_bounds")


def pick(tiles, lane, high, first):
    found = lane_take(tiles[0], lane)
    for j in range(1, len(tiles)):
        found = jnp.where(high == first + j, lane_take(tiles[j], lane), found)
    return found


def spread8(row):
    return jnp.broadcast_to(row, (8, row.shape[1]))


def split_index(index):
    return lax.bitwise_and(index, LANES - 1), lax.shift_right_logical(index, 7)


def kernel(
    n_cells, n_spec,
    damping, block_count, *refs,
):
    count = len(LOADED)
    given, (wind_out, spectra_out), held = refs[:count], refs[count:count + 2], refs[count + 2:2 * count + 2]
    (wind, atm_send, spectra, sea_mask, atm_table, atm_coef, recv_cells, ocn_send, face_angle, face_ratio, slot_weight,
     send_cells, ocn_table) = held
    (ext1, ext2, rim1, rim2, surf, blk_send, blk_recv, onehot, onehot_rim, near_recv, near_send, means_own, means,
     trig, faces, ocn_rim, ocn_ext,
     load_sem, atm_ssem, atm_rsem, mean_ssem, mean_rsem, surf_ssem, surf_rsem, blk_ssem, blk_rsem, ocn_ssem, ocn_rsem,
     near_ssem, near_rsem) = refs[2 * count + 2:]
    me = lax.axis_index("cells")
    part = lax.axis_index("spec")
    before, after = lax.rem(me + n_cells - 1, n_cells), lax.rem(me + 1, n_cells)
    levels, cells = wind.shape[1], wind.shape[2]
    own_tiles = cells // LANES
    rim = rim1.shape[2]
    rim_tiles = rim // LANES
    bands, ocean = spectra.shape[0], spectra.shape[2]
    ocean_tiles = ocean // LANES
    slots = send_cells.shape[1]
    stored = n_cells <= 16

    barrier = pltpu.get_barrier_semaphore()

    def greet_cells(step, carry):
        other = lax.rem(me + step, n_cells)
        pl.semaphore_signal(barrier, inc=1, device_id=(other, part), device_id_type=MESH)
        return carry

    def greet_spec(step, carry):
        other = lax.rem(part + step, n_spec)
        pl.semaphore_signal(barrier, inc=1, device_id=(me, other), device_id_type=MESH)
        return carry

    lax.fori_loop(1, n_cells, greet_cells, 0)
    lax.fori_loop(1, n_spec, greet_spec, 0)

    loads = [pltpu.make_async_copy(given[q], held[q], load_sem.at[q]) for q in range(count)]
    for load in loads:
        load.start()

    def gather_rim(ext, out):
        tiles = [ext[:, pl.ds(rim + j * LANES, LANES)] for j in range(own_tiles)]
        for t in range(2 * rim_tiles):
            lane, high = split_index(spread8(atm_send[pl.ds(t, 1), :]))
            out[t // rim_tiles, :, pl.ds((t % rim_tiles) * LANES, LANES)] = pick(tiles, lane, high, 0)

    def rim_copies(out, ext, base):
        to_before = pltpu.make_async_remote_copy(
            src_ref=out.at[0], dst_ref=ext.at[:, pl.ds(rim + cells, rim)],
            send_sem=atm_ssem.at[base], recv_sem=atm_rsem.at[base],
            device_id=(before, part), device_id_type=MESH)
        to_after = pltpu.make_async_remote_copy(
            src_ref=out.at[1], dst_ref=ext.at[:, pl.ds(0, rim)],
            send_sem=atm_ssem.at[base + 1], recv_sem=atm_rsem.at[base + 1],
            device_id=(after, part), device_id_type=MESH)
        return to_before, to_after

    def laplace(ext, store):
        def block(b, carry):
            start = pl.multiple_of(b * LANES, LANES)
            here = ext[:, pl.ds(rim + start, LANES)]
            tiles = [ext[:, pl.ds(start + j * LANES, LANES)] for j in range(2 * rim_tiles + 1)]
            total = jnp.zeros((8, LANES), jnp.float32)
            for k in range(3):
                lane, high = split_index(spread8(atm_table[pl.ds(k, 1), pl.ds(start, LANES)]))
                near = pick(tiles, lane, high - b, 0)
                total += spread8(atm_coef[pl.ds(k, 1), pl.ds(start, LANES)]) * (near - here)
            store(start, here, total)
            return carry

        lax.fori_loop(0, own_tiles, block, 0, unroll=4)

    for load in loads[:2]:
        load.wait()
    ext1[0:levels, pl.ds(rim, cells)] = wind[0]
    ext1[levels:2 * levels, pl.ds(rim, cells)] = wind[1]
    gather_rim(ext1, rim1)
    pl.semaphore_wait(barrier, n_cells + n_spec - 2)
    first = rim_copies(rim1, ext1, 0)
    for copy in first:
        copy.start()

    for load in loads[2:]:
        load.wait()

    def near_copies(side, other):
        at = 1 - side
        return [
            pltpu.make_async_remote_copy(
                src_ref=src, dst_ref=dst.at[at], send_sem=near_ssem.at[2 * at + q], recv_sem=near_rsem.at[2 * at + q],
                device_id=(other, part), device_id_type=MESH)
            for q, (src, dst) in enumerate(((recv_cells, near_recv), (ocn_send, near_send)))
        ]

    near = near_copies(0, before) + near_copies(1, after)
    for copy in near:
        copy.start()

    mask = sea_mask[...].astype(jnp.float32)
    frequency = []
    for k in range(bands):
        value = jnp.float32(0.6 * 1.1**k)
        for s in range(1, n_spec):
            value = jnp.where(part == s, jnp.float32(0.6 * 1.1 ** (s * bands + k)), value)
        frequency.append(value)
    total = jnp.zeros((1, ocean), jnp.float32)
    inverse = jnp.zeros((1, ocean), jnp.float32)
    for k in range(bands):
        band_sum = jnp.sum(spectra[k] * mask, axis=0, keepdims=True)
        total += band_sum
        inverse += band_sum * (1.0 / jnp.full((1, ocean), frequency[k], jnp.float32))
    means_own[0:1, :] = total
    means_own[1:2, :] = inverse

    def mean_copy(other, slot):
        return pltpu.make_async_remote_copy(
            src_ref=means_own, dst_ref=means.at[slot],
            send_sem=mean_ssem.at[other], recv_sem=mean_rsem.at[slot],
            device_id=(me, other), device_id_type=MESH)

    for step in range(1, n_spec):
        mean_copy(lax.rem(part + step, n_spec), part).start()

    for copy in first:
        copy.wait_recv()

    def keep_once(start, here, lap):
        ext2[:, pl.ds(rim + start, LANES)] = lap

    laplace(ext1, keep_once)
    gather_rim(ext2, rim2)
    second = rim_copies(rim2, ext2, 2)
    for copy in second:
        copy.start()

    def hits(i):
        place = lax.broadcasted_iota(jnp.int32, (ocean, slots), 0)
        return jnp.where(place == recv_cells[pl.ds(i, 1), :], 1.0, 0.0).astype(jnp.bfloat16)

    def rim_hits(side, column, i):
        return jnp.where(column == near_recv[side, pl.ds(i, 1), :], 1.0, 0.0).astype(jnp.bfloat16)

    for copy in near:
        copy.wait_recv()
    columns = []
    for side in range(2):
        names = near_send[side, 1 - side:2 - side, :].astype(jnp.float32)
        column = jnp.transpose(jnp.broadcast_to(names, (LANES, LANES))).astype(jnp.int32)
        columns.append(jnp.concatenate([column] * (slots // LANES), axis=1))
    if stored:
        for i in range(n_cells):
            at = slice(i * slots, (i + 1) * slots)
            onehot[:, at] = hits(i)
            for side in range(2):
                onehot_rim[side, :, at] = rim_hits(side, columns[side], i)
    heading = (lax.broadcasted_iota(jnp.int32, (ROWS, LANES), 0).astype(jnp.float32) + 0.5) * (
        2.0 * math.pi / DIRECTIONS
    )
    trig[0] = jnp.cos(heading)
    trig[1] = jnp.sin(heading)
    angle = face_angle[...]
    ratio = face_ratio[...]
    faces[0] = jnp.cos(angle) * ratio
    faces[1] = jnp.sin(angle) * ratio
    total = means_own[0:1, :]
    inverse = means_own[1:2, :]
    for step in range(1, n_spec):
        other = lax.rem(part + step, n_spec)
        mean_copy(other, other).wait_recv()
        total += means[other, 0:1, :]
        inverse += means[other, 1:2, :]
    components = DIRECTIONS * BANDS
    mean_energy = total / components
    mean_freq = mean_energy / (inverse / components + epsilon)
    squared = mean_freq * mean_freq
    for k in range(bands):
        decay = (dissipation * frequency[k]) * (mean_energy * (squared * squared))
        own = pl.ds(LANES, ocean)
        ocn_ext[k * ROWS + 32:(k + 1) * ROWS, own] = jnp.zeros((8, ocean), jnp.float32)
        ocn_ext[k * ROWS:k * ROWS + DIRECTIONS, own] = spectra[k] * (mask * (1.0 / (1.0 + decay)))
    for side in range(2):
        lane, high = split_index(spread8(ocn_send[side:side + 1, :]))
        for r in range(bands * ROWS // 8):
            rows = slice(r * 8, r * 8 + 8)
            tiles = [ocn_ext[rows, LANES + j * LANES:LANES + (j + 1) * LANES] for j in range(ocean_tiles)]
            ocn_rim[side, rows, :] = pick(tiles, lane, high, 0)
    third = (
        pltpu.make_async_remote_copy(
            src_ref=ocn_rim.at[0], dst_ref=ocn_ext.at[:, pl.ds(ocean + LANES, LANES)],
            send_sem=ocn_ssem.at[0], recv_sem=ocn_rsem.at[0],
            device_id=(before, part), device_id_type=MESH),
        pltpu.make_async_remote_copy(
            src_ref=ocn_rim.at[1], dst_ref=ocn_ext.at[:, pl.ds(0, LANES)],
            send_sem=ocn_ssem.at[1], recv_sem=ocn_rsem.at[1],
            device_id=(after, part), device_id_type=MESH),
    )
    for copy in third:
        copy.start()

    for copy in second:
        copy.wait_recv()
    row = lax.broadcasted_iota(jnp.int32, (8, LANES), 0)
    rate = jnp.zeros((8, LANES), jnp.float32)
    for v in range(levels):
        rate = jnp.where(lax.rem(row, levels) == v, damping[v], rate)

    def keep_damped(start, here, lap):
        damped = ext1[:, pl.ds(rim + start, LANES)] - rate * lap
        wind_out[0, :, pl.ds(start, LANES)] = damped[0:levels]
        wind_out[1, :, pl.ds(start, LANES)] = damped[levels:2 * levels]

    laplace(ext2, keep_damped)

    def surf_copy(other):
        return pltpu.make_async_remote_copy(
            src_ref=surf, dst_ref=surf, send_sem=surf_ssem.at[other], recv_sem=surf_rsem,
            device_id=(me, other), device_id_type=MESH)

    @pl.when(part == n_spec - 1)
    def _():
        surf[0:1, :] = wind_factor * wind_out[0, levels - 1:levels, :]
        surf[1:2, :] = wind_factor * wind_out[1, levels - 1:levels, :]
        for other in range(n_spec - 1):
            surf_copy(other).start()

    @pl.when(part != n_spec - 1)
    def _():
        surf_copy(0).wait_recv()

    for g in range(n_cells // 8):
        row = lax.broadcasted_iota(jnp.int32, (8, LANES), 0)
        live = jnp.zeros((8, LANES), jnp.int32)
        for i in range(8):
            live = jnp.where(row == i, block_count[g * 8 + i], live)
        for h in range(slots // LANES):
            spot = lax.broadcasted_iota(jnp.int32, (8, LANES), 1) + h * LANES
            scale = jnp.where(spot < live, slot_weight[g * 8:g * 8 + 8, pl.ds(h * LANES, LANES)], 0.0)
            lane, high = split_index(send_cells[g * 8:g * 8 + 8, pl.ds(h * LANES, LANES)])
            for c in range(2):
                tiles = [spread8(surf[c:c + 1, pl.ds(j * LANES, LANES)]) for j in range(own_tiles)]
                blk_send[g * 8 + 1:g * 8 + 9, c, pl.ds(h * LANES, LANES)] = scale * pick(tiles, lane, high, 0)

    blk_send[0] = blk_send[n_cells]
    blk_send[n_cells + 1] = blk_send[1]

    def block_copy(other, slot):
        return pltpu.make_async_remote_copy(
            src_ref=blk_send.at[pl.ds(other, 3)], dst_ref=blk_recv.at[slot],
            send_sem=blk_ssem.at[other], recv_sem=blk_rsem.at[slot],
            device_id=(other, part), device_id_type=MESH)

    def send_block(step, carry):
        block_copy(lax.rem(me + step, n_cells), me).start()
        return carry

    lax.fori_loop(1, n_cells, send_block, 0)
    for r in range(3):
        blk_recv[me, r] = blk_send[me + r]

    def wait_block(step, carry):
        other = lax.rem(me + step, n_cells)
        block_copy(other, other).wait_recv()
        return carry

    lax.fori_loop(1, n_cells, wait_block, 0)

    def product(value, ones):
        high = value.astype(jnp.bfloat16).astype(jnp.float32)
        rest = value - high
        middle = rest.astype(jnp.bfloat16).astype(jnp.float32)
        parts = jnp.concatenate([high, middle, rest - middle, jnp.zeros_like(high)], axis=0)
        return lax.dot_general(
            parts.astype(jnp.bfloat16), ones, (((1,), (1,)), ((), ())), preferred_element_type=jnp.float32)

    def deposit(i, sums):
        if stored:
            at = slice(i * slots, (i + 1) * slots)
            ones = [onehot_rim[0, :, at], onehot[:, at], onehot_rim[1, :, at]]
        else:
            ones = [rim_hits(0, columns[0], i), hits(i), rim_hits(1, columns[1], i)]
        return tuple(acc + product(blk_recv[i, r], ones[r]) for r, acc in enumerate(sums))

    sums = tuple(jnp.zeros((8, width), jnp.float32) for width in (LANES, ocean, LANES))
    if stored:
        for i in range(n_cells):
            sums = deposit(i, sums)
    else:
        sums = lax.fori_loop(0, n_cells, deposit, sums)
    acc = jnp.concatenate(sums, axis=1)
    wind_u = acc[0:1] + acc[2:3] + acc[4:5]
    wind_v = acc[1:2] + acc[3:4] + acc[5:6]

    for copy in third:
        copy.wait_recv()
    for g in range(ROWS // 8):
        rows = slice(g * 8, g * 8 + 8)
        for b in range(ocean_tiles + 2):
            at = slice(b * LANES, (b + 1) * LANES)
            along = trig[0, rows, :] * wind_u[:, at] + trig[1, rows, :] * wind_v[:, at]
            for k in range(bands):
                gain = (growth * frequency[k]) * jnp.maximum((coupling * frequency[k]) * along - 1.0, 0.0)
                spot = slice(k * ROWS + g * 8, k * ROWS + g * 8 + 8)
                ocn_ext[spot, at] = ocn_ext[spot, at] * (1.0 + gain)

    for b in range(ocean_tiles):
        at = slice(b * LANES, (b + 1) * LANES)
        index = [split_index(spread8(ocn_table[f:f + 1, at])) for f in range(3)]
        for g in range(ROWS // 8):
            normal = [
                trig[0, g * 8:g * 8 + 8, :] * faces[0, f:f + 1, at] + trig[1, g * 8:g * 8 + 8, :] * faces[1, f:f + 1, at]
                for f in range(3)
            ]
            for k in range(bands):
                speed = 0.5 / jnp.full((8, LANES), frequency[k], jnp.float32)
                rows = slice(k * ROWS + g * 8, k * ROWS + g * 8 + 8)
                tiles = [ocn_ext[rows, (b + j) * LANES:(b + j + 1) * LANES] for j in range(3)]
                here = tiles[1]
                result = here
                for f in range(3):
                    transport = speed * normal[f]
                    upwind = pick(tiles, index[f][0], index[f][1], b)
                    result = result - transport * jnp.where(transport > 0.0, here, upwind)
                size = min(8, DIRECTIONS - g * 8)
                spectra_out[k, g * 8:g * 8 + size, at] = result[0:size]
    for copy in (*first, *second, *third, *near):
        copy.wait_send()
    for step in range(1, n_spec):
        mean_copy(lax.rem(part + step, n_spec), part).wait_send()

    @pl.when(part == n_spec - 1)
    def _():
        for other in range(n_spec - 1):
            surf_copy(other).wait_send()

    def sent_block(step, carry):
        block_copy(lax.rem(me + step, n_cells), me).wait_send()
        return carry

    lax.fori_loop(1, n_cells, sent_block, 0)


def local(
    n_cells, n_spec,
    wind_field, damping, atm_table, atm_coef, atm_send, send_cells, block_count, slot_weight, recv_cells,
    spectra, sea_mask, ocn_table, face_angle, face_ratio, ocn_send,
):
    levels, cells = wind_field.shape[1:]
    rim = atm_send.shape[0] // 2
    bands, ocean = spectra.shape[1:]
    slots = send_cells.shape[1]
    f32 = jnp.float32
    vmem = pl.BlockSpec(memory_space=pltpu.VMEM)
    smem = pl.BlockSpec(memory_space=pltpu.SMEM)
    hbm = pl.BlockSpec(memory_space=pltpu.HBM)
    dma = pltpu.SemaphoreType.DMA
    loaded = dict(
        wind=wind_field, atm_send=atm_send.reshape(-1, LANES), spectra=jnp.transpose(spectra, (1, 0, 2)),
        sea_mask=sea_mask.reshape(1, -1), atm_table=atm_table, atm_coef=atm_coef, recv_cells=recv_cells,
        ocn_send=ocn_send.reshape(-1, LANES), face_angle=face_angle, face_ratio=face_ratio, slot_weight=slot_weight,
        send_cells=send_cells, ocn_table=ocn_table,
    )
    loaded = [loaded[name] for name in LOADED]
    held_slots = n_cells * slots if n_cells <= 16 else LANES
    wind_out, spectra_out = pl.pallas_call(
        functools.partial(kernel, n_cells, n_spec),
        out_shape=(
            jax.ShapeDtypeStruct(wind_field.shape, f32),
            jax.ShapeDtypeStruct((bands, DIRECTIONS, ocean), f32),
        ),
        in_specs=[smem, smem] + [hbm] * len(loaded),
        out_specs=(vmem, vmem),
        scratch_shapes=[
            *(pltpu.VMEM(array.shape, array.dtype) for array in loaded),
            pltpu.VMEM((2 * levels, cells + 2 * rim), f32),
            pltpu.VMEM((2 * levels, cells + 2 * rim), f32),
            pltpu.VMEM((2, 2 * levels, rim), f32),
            pltpu.VMEM((2, 2 * levels, rim), f32),
            pltpu.VMEM((2, cells), f32),
            pltpu.VMEM((n_cells + 2, 2, slots), f32),
            pltpu.VMEM((n_cells, 3, 2, slots), f32),
            pltpu.VMEM((ocean, held_slots), jnp.bfloat16),
            pltpu.VMEM((2, LANES, held_slots), jnp.bfloat16),
            pltpu.VMEM((2, n_cells, slots), jnp.int32),
            pltpu.VMEM((2, 2, LANES), jnp.int32),
            pltpu.VMEM((2, ocean), f32),
            pltpu.VMEM((n_spec, 2, ocean), f32),
            pltpu.VMEM((2, ROWS, LANES), f32),
            pltpu.VMEM((2, 3, ocean), f32),
            pltpu.VMEM((2, bands * ROWS, LANES), f32),
            pltpu.VMEM((bands * ROWS, ocean + 2 * LANES), f32),
            dma((len(loaded),)), dma((4,)), dma((4,)), dma((n_spec,)), dma((n_spec,)), dma((n_spec,)), dma,
            dma((n_cells,)), dma((n_cells,)), dma((2,)), dma((2,)), dma((4,)), dma((4,)),
        ],
        compiler_params=pltpu.CompilerParams(
            collective_id=0, has_side_effects=True, vmem_limit_bytes=60 * 2**20
        ),
    )(damping, block_count, *loaded)
    return wind_out, jnp.transpose(spectra_out, (1, 0, 2))


def solution(mesh):
    in_specs = (
        P(None, "spec", "cells"),
        P("spec"),
        P(None, "cells"),
        P(None, "cells"),
        P("cells"),
        P("cells", None),
        P("cells"),
        P("cells", None),
        P("cells", None),
        P(None, "spec", "cells"),
        P("cells"),
        P(None, "cells"),
        P(None, "cells"),
        P(None, "cells"),
        P("cells"),
    )
    out_specs = (P(None, "spec", "cells"), P(None, "spec", "cells"))
    body = functools.partial(local, mesh.shape["cells"], mesh.shape["spec"])
    return jax.shard_map(body, mesh=mesh, in_specs=in_specs, out_specs=out_specs, check_vma=False)
```

```python
import functools
import math

import jax
import jax.numpy as jnp
from jax import lax
from jax.experimental import pallas as pl
from jax.experimental.pallas import tpu as pltpu
from jax.sharding import PartitionSpec as P

DIRECTIONS = 36
BANDS = 12
ROWS = 40
LANES = 128
MESH = pl.DeviceIdType.MESH
LOADED = (
    "wind", "atm_send", "spectra", "sea_mask", "atm_table", "atm_coef", "recv_cells", "ocn_send", "face_angle",
    "face_ratio", "slot_weight", "send_cells", "ocn_table", "damping", "block_count",
)

epsilon = 1e-06
wind_factor = 0.8
growth = 0.1
coupling = 4.0
dissipation = 0.05


def lane_take(tile, lane):
    return jnp.take_along_axis(tile, lane, axis=1, mode="promise_in_bounds")


def pick(tiles, lane, high, first):
    found = lane_take(tiles[0], lane)
    for j in range(1, len(tiles)):
        found = jnp.where(high == first + j, lane_take(tiles[j], lane), found)
    return found


def spread8(row):
    return jnp.broadcast_to(row, (8, row.shape[1]))


def split_index(index):
    return lax.bitwise_and(index, LANES - 1), lax.shift_right_logical(index, 7)


def kernel(
    n_cells, n_spec,
    *refs,
):
    count = len(LOADED)
    given, (wind_out, spectra_out), held = refs[:count], refs[count:count + 2], refs[count + 2:2 * count + 2]
    (wind, atm_send, spectra, sea_mask, atm_table, atm_coef, recv_cells, ocn_send, face_angle, face_ratio, slot_weight,
     send_cells, ocn_table, damping, block_count) = held
    (ext1, ext2, rim1, rim2, surf, blk_send, blk_recv, onehot, onehot_rim, near_recv, near_send, means_own, means,
     trig, faces, ocn_rim, ocn_ext,
     load_sem, atm_ssem, atm_rsem, mean_ssem, mean_rsem, surf_ssem, surf_rsem, blk_ssem, blk_rsem, ocn_ssem, ocn_rsem,
     near_ssem, near_rsem) = refs[2 * count + 2:]
    me = lax.axis_index("cells")
    part = lax.axis_index("spec")
    before, after = lax.rem(me + n_cells - 1, n_cells), lax.rem(me + 1, n_cells)
    levels, cells = wind.shape[1], wind.shape[2]
    own_tiles = cells // LANES
    rim = rim1.shape[2]
    rim_tiles = rim // LANES
    bands, ocean = spectra.shape[0], spectra.shape[2]
    ocean_tiles = ocean // LANES
    slots = send_cells.shape[1]
    stored = n_cells <= 16

    barrier = pltpu.get_barrier_semaphore()

    def greet_cells(step, carry):
        other = lax.rem(me + step, n_cells)
        pl.semaphore_signal(barrier, inc=1, device_id=(other, part), device_id_type=MESH)
        return carry

    def greet_spec(step, carry):
        other = lax.rem(part + step, n_spec)
        pl.semaphore_signal(barrier, inc=1, device_id=(me, other), device_id_type=MESH)
        return carry

    lax.fori_loop(1, n_cells, greet_cells, 0)
    lax.fori_loop(1, n_spec, greet_spec, 0)

    loads = [pltpu.make_async_copy(given[q], held[q], load_sem.at[q]) for q in range(count)]
    for load in loads:
        load.start()

    def gather_rim(ext, out):
        tiles = [ext[:, pl.ds(rim + j * LANES, LANES)] for j in range(own_tiles)]
        for t in range(2 * rim_tiles):
            lane, high = split_index(spread8(atm_send[pl.ds(t, 1), :]))
            out[t // rim_tiles, :, pl.ds((t % rim_tiles) * LANES, LANES)] = pick(tiles, lane, high, 0)

    def rim_copies(out, ext, base):
        to_before = pltpu.make_async_remote_copy(
            src_ref=out.at[0], dst_ref=ext.at[:, pl.ds(rim + cells, rim)],
            send_sem=atm_ssem.at[base], recv_sem=atm_rsem.at[base],
            device_id=(before, part), device_id_type=MESH)
        to_after = pltpu.make_async_remote_copy(
            src_ref=out.at[1], dst_ref=ext.at[:, pl.ds(0, rim)],
            send_sem=atm_ssem.at[base + 1], recv_sem=atm_rsem.at[base + 1],
            device_id=(after, part), device_id_type=MESH)
        return to_before, to_after

    def laplace(ext, store):
        def block(b, carry):
            start = pl.multiple_of(b * LANES, LANES)
            here = ext[:, pl.ds(rim + start, LANES)]
            tiles = [ext[:, pl.ds(start + j * LANES, LANES)] for j in range(2 * rim_tiles + 1)]
            total = jnp.zeros((8, LANES), jnp.float32)
            for k in range(3):
                lane, high = split_index(spread8(atm_table[pl.ds(k, 1), pl.ds(start, LANES)]))
                near = pick(tiles, lane, high - b, 0)
                total += spread8(atm_coef[pl.ds(k, 1), pl.ds(start, LANES)]) * (near - here)
            store(start, here, total)
            return carry

        lax.fori_loop(0, own_tiles, block, 0, unroll=4)

    for load in loads[:2]:
        load.wait()
    ext1[0:levels, pl.ds(rim, cells)] = wind[0]
    ext1[levels:2 * levels, pl.ds(rim, cells)] = wind[1]
    gather_rim(ext1, rim1)
    pl.semaphore_wait(barrier, n_cells + n_spec - 2)
    first = rim_copies(rim1, ext1, 0)
    for copy in first:
        copy.start()

    for load in loads[2:]:
        load.wait()

    def near_copies(side, other):
        at = 1 - side
        return [
            pltpu.make_async_remote_copy(
                src_ref=src, dst_ref=dst.at[at], send_sem=near_ssem.at[2 * at + q], recv_sem=near_rsem.at[2 * at + q],
                device_id=(other, part), device_id_type=MESH)
            for q, (src, dst) in enumerate(((recv_cells, near_recv), (ocn_send, near_send)))
        ]

    near = near_copies(0, before) + near_copies(1, after)
    for copy in near:
        copy.start()

    mask = sea_mask[...].astype(jnp.float32)
    frequency = []
    for k in range(bands):
        value = jnp.float32(0.6 * 1.1**k)
        for s in range(1, n_spec):
            value = jnp.where(part == s, jnp.float32(0.6 * 1.1 ** (s * bands + k)), value)
        frequency.append(value)
    total = jnp.zeros((1, ocean), jnp.float32)
    inverse = jnp.zeros((1, ocean), jnp.float32)
    for k in range(bands):
        band_sum = jnp.sum(spectra[k] * mask, axis=0, keepdims=True)
        total += band_sum
        inverse += band_sum * (1.0 / jnp.full((1, ocean), frequency[k], jnp.float32))
    means_own[0:1, :] = total
    means_own[1:2, :] = inverse

    def mean_copy(other, slot):
        return pltpu.make_async_remote_copy(
            src_ref=means_own, dst_ref=means.at[slot],
            send_sem=mean_ssem.at[other], recv_sem=mean_rsem.at[slot],
            device_id=(me, other), device_id_type=MESH)

    for step in range(1, n_spec):
        mean_copy(lax.rem(part + step, n_spec), part).start()

    for copy in first:
        copy.wait_recv()

    def keep_once(start, here, lap):
        ext2[:, pl.ds(rim + start, LANES)] = lap

    laplace(ext1, keep_once)
    gather_rim(ext2, rim2)
    second = rim_copies(rim2, ext2, 2)
    for copy in second:
        copy.start()

    def hits(i):
        place = lax.broadcasted_iota(jnp.int32, (ocean, slots), 0)
        return jnp.where(place == recv_cells[pl.ds(i, 1), :], 1.0, 0.0).astype(jnp.bfloat16)

    def rim_hits(side, column, i):
        return jnp.where(column == near_recv[side, pl.ds(i, 1), :], 1.0, 0.0).astype(jnp.bfloat16)

    for copy in near:
        copy.wait_recv()
    columns = []
    for side in range(2):
        names = near_send[side, 1 - side:2 - side, :].astype(jnp.float32)
        column = jnp.transpose(jnp.broadcast_to(names, (LANES, LANES))).astype(jnp.int32)
        columns.append(jnp.concatenate([column] * (slots // LANES), axis=1))
    if stored:
        for i in range(n_cells):
            at = slice(i * slots, (i + 1) * slots)
            onehot[:, at] = hits(i)
            for side in range(2):
                onehot_rim[side, :, at] = rim_hits(side, columns[side], i)
    heading = (lax.broadcasted_iota(jnp.int32, (ROWS, LANES), 0).astype(jnp.float32) + 0.5) * (
        2.0 * math.pi / DIRECTIONS
    )
    trig[0] = jnp.cos(heading)
    trig[1] = jnp.sin(heading)
    angle = face_angle[...]
    ratio = face_ratio[...]
    faces[0] = jnp.cos(angle) * ratio
    faces[1] = jnp.sin(angle) * ratio
    total = means_own[0:1, :]
    inverse = means_own[1:2, :]
    for step in range(1, n_spec):
        other = lax.rem(part + step, n_spec)
        mean_copy(other, other).wait_recv()
        total += means[other, 0:1, :]
        inverse += means[other, 1:2, :]
    components = DIRECTIONS * BANDS
    mean_energy = total / components
    mean_freq = mean_energy / (inverse / components + epsilon)
    squared = mean_freq * mean_freq
    for k in range(bands):
        decay = (dissipation * frequency[k]) * (mean_energy * (squared * squared))
        own = pl.ds(LANES, ocean)
        ocn_ext[k * ROWS + 32:(k + 1) * ROWS, own] = jnp.zeros((8, ocean), jnp.float32)
        ocn_ext[k * ROWS:k * ROWS + DIRECTIONS, own] = spectra[k] * (mask * (1.0 / (1.0 + decay)))
    for side in range(2):
        lane, high = split_index(spread8(ocn_send[side:side + 1, :]))
        for r in range(bands * ROWS // 8):
            rows = slice(r * 8, r * 8 + 8)
            tiles = [ocn_ext[rows, LANES + j * LANES:LANES + (j + 1) * LANES] for j in range(ocean_tiles)]
            ocn_rim[side, rows, :] = pick(tiles, lane, high, 0)
    third = (
        pltpu.make_async_remote_copy(
            src_ref=ocn_rim.at[0], dst_ref=ocn_ext.at[:, pl.ds(ocean + LANES, LANES)],
            send_sem=ocn_ssem.at[0], recv_sem=ocn_rsem.at[0],
            device_id=(before, part), device_id_type=MESH),
        pltpu.make_async_remote_copy(
            src_ref=ocn_rim.at[1], dst_ref=ocn_ext.at[:, pl.ds(0, LANES)],
            send_sem=ocn_ssem.at[1], recv_sem=ocn_rsem.at[1],
            device_id=(after, part), device_id_type=MESH),
    )
    for copy in third:
        copy.start()

    for copy in second:
        copy.wait_recv()
    row = lax.broadcasted_iota(jnp.int32, (8, LANES), 0)
    rate = jnp.zeros((8, LANES), jnp.float32)
    for v in range(levels):
        rate = jnp.where(lax.rem(row, levels) == v, damping[v], rate)

    def keep_damped(start, here, lap):
        damped = ext1[:, pl.ds(rim + start, LANES)] - rate * lap
        wind_out[0, :, pl.ds(start, LANES)] = damped[0:levels]
        wind_out[1, :, pl.ds(start, LANES)] = damped[levels:2 * levels]

    laplace(ext2, keep_damped)

    def surf_copy(other):
        return pltpu.make_async_remote_copy(
            src_ref=surf, dst_ref=surf, send_sem=surf_ssem.at[other], recv_sem=surf_rsem,
            device_id=(me, other), device_id_type=MESH)

    @pl.when(part == n_spec - 1)
    def _():
        surf[0:1, :] = wind_factor * wind_out[0, levels - 1:levels, :]
        surf[1:2, :] = wind_factor * wind_out[1, levels - 1:levels, :]
        for other in range(n_spec - 1):
            surf_copy(other).start()

    @pl.when(part != n_spec - 1)
    def _():
        surf_copy(0).wait_recv()

    for g in range(n_cells // 8):
        row = lax.broadcasted_iota(jnp.int32, (8, LANES), 0)
        live = jnp.zeros((8, LANES), jnp.int32)
        for i in range(8):
            live = jnp.where(row == i, block_count[g * 8 + i], live)
        for h in range(slots // LANES):
            spot = lax.broadcasted_iota(jnp.int32, (8, LANES), 1) + h * LANES
            scale = jnp.where(spot < live, slot_weight[g * 8:g * 8 + 8, pl.ds(h * LANES, LANES)], 0.0)
            lane, high = split_index(send_cells[g * 8:g * 8 + 8, pl.ds(h * LANES, LANES)])
            for c in range(2):
                tiles = [spread8(surf[c:c + 1, pl.ds(j * LANES, LANES)]) for j in range(own_tiles)]
                blk_send[g * 8 + 1:g * 8 + 9, c, pl.ds(h * LANES, LANES)] = scale * pick(tiles, lane, high, 0)

    blk_send[0] = blk_send[n_cells]
    blk_send[n_cells + 1] = blk_send[1]

    def block_copy(other, slot):
        return pltpu.make_async_remote_copy(
            src_ref=blk_send.at[pl.ds(other, 3)], dst_ref=blk_recv.at[slot],
            send_sem=blk_ssem.at[other], recv_sem=blk_rsem.at[slot],
            device_id=(other, part), device_id_type=MESH)

    def send_block(step, carry):
        block_copy(lax.rem(me + step, n_cells), me).start()
        return carry

    lax.fori_loop(1, n_cells, send_block, 0)
    for r in range(3):
        blk_recv[me, r] = blk_send[me + r]

    def wait_block(step, carry):
        other = lax.rem(me + step, n_cells)
        block_copy(other, other).wait_recv()
        return carry

    lax.fori_loop(1, n_cells, wait_block, 0)

    def product(value, ones):
        high = value.astype(jnp.bfloat16).astype(jnp.float32)
        rest = value - high
        middle = rest.astype(jnp.bfloat16).astype(jnp.float32)
        parts = jnp.concatenate([high, middle, rest - middle, jnp.zeros_like(high)], axis=0)
        return lax.dot_general(
            parts.astype(jnp.bfloat16), ones, (((1,), (1,)), ((), ())), preferred_element_type=jnp.float32)

    def deposit(i, sums):
        if stored:
            at = slice(i * slots, (i + 1) * slots)
            ones = [onehot_rim[0, :, at], onehot[:, at], onehot_rim[1, :, at]]
        else:
            ones = [rim_hits(0, columns[0], i), hits(i), rim_hits(1, columns[1], i)]
        return tuple(acc + product(blk_recv[i, r], ones[r]) for r, acc in enumerate(sums))

    sums = tuple(jnp.zeros((8, width), jnp.float32) for width in (LANES, ocean, LANES))
    if stored:
        for i in range(n_cells):
            sums = deposit(i, sums)
    else:
        sums = lax.fori_loop(0, n_cells, deposit, sums)
    acc = jnp.concatenate(sums, axis=1)
    wind_u = acc[0:1] + acc[2:3] + acc[4:5]
    wind_v = acc[1:2] + acc[3:4] + acc[5:6]

    for copy in third:
        copy.wait_recv()
    for g in range(ROWS // 8):
        rows = slice(g * 8, g * 8 + 8)
        for b in range(ocean_tiles + 2):
            at = slice(b * LANES, (b + 1) * LANES)
            along = trig[0, rows, :] * wind_u[:, at] + trig[1, rows, :] * wind_v[:, at]
            for k in range(bands):
                gain = (growth * frequency[k]) * jnp.maximum((coupling * frequency[k]) * along - 1.0, 0.0)
                spot = slice(k * ROWS + g * 8, k * ROWS + g * 8 + 8)
                ocn_ext[spot, at] = ocn_ext[spot, at] * (1.0 + gain)

    for b in range(ocean_tiles):
        at = slice(b * LANES, (b + 1) * LANES)
        index = [split_index(spread8(ocn_table[f:f + 1, at])) for f in range(3)]
        for g in range(ROWS // 8):
            normal = [
                trig[0, g * 8:g * 8 + 8, :] * faces[0, f:f + 1, at] + trig[1, g * 8:g * 8 + 8, :] * faces[1, f:f + 1, at]
                for f in range(3)
            ]
            for k in range(bands):
                speed = 0.5 / jnp.full((8, LANES), frequency[k], jnp.float32)
                rows = slice(k * ROWS + g * 8, k * ROWS + g * 8 + 8)
                tiles = [ocn_ext[rows, (b + j) * LANES:(b + j + 1) * LANES] for j in range(3)]
                here = tiles[1]
                result = here
                for f in range(3):
                    transport = speed * normal[f]
                    upwind = pick(tiles, index[f][0], index[f][1], b)
                    result = result - transport * jnp.where(transport > 0.0, here, upwind)
                size = min(8, DIRECTIONS - g * 8)
                spectra_out[k, g * 8:g * 8 + size, at] = result[0:size]
    for copy in (*first, *second, *third, *near):
        copy.wait_send()
    for step in range(1, n_spec):
        mean_copy(lax.rem(part + step, n_spec), part).wait_send()

    @pl.when(part == n_spec - 1)
    def _():
        for other in range(n_spec - 1):
            surf_copy(other).wait_send()

    def sent_block(step, carry):
        block_copy(lax.rem(me + step, n_cells), me).wait_send()
        return carry

    lax.fori_loop(1, n_cells, sent_block, 0)


def local(
    n_cells, n_spec,
    wind_field, damping, atm_table, atm_coef, atm_send, send_cells, block_count, slot_weight, recv_cells,
    spectra, sea_mask, ocn_table, face_angle, face_ratio, ocn_send,
):
    levels, cells = wind_field.shape[1:]
    rim = atm_send.shape[0] // 2
    bands, ocean = spectra.shape[1:]
    slots = send_cells.shape[1]
    f32 = jnp.float32
    vmem = pl.BlockSpec(memory_space=pltpu.VMEM)
    hbm = pl.BlockSpec(memory_space=pltpu.HBM)
    dma = pltpu.SemaphoreType.DMA
    loaded = dict(
        wind=wind_field, atm_send=atm_send.reshape(-1, LANES), spectra=jnp.transpose(spectra, (1, 0, 2)),
        sea_mask=sea_mask.reshape(1, -1), atm_table=atm_table, atm_coef=atm_coef, recv_cells=recv_cells,
        ocn_send=ocn_send.reshape(-1, LANES), face_angle=face_angle, face_ratio=face_ratio, slot_weight=slot_weight,
        send_cells=send_cells, ocn_table=ocn_table, damping=damping, block_count=block_count,
    )
    loaded = [pltpu.with_memory_space_constraint(loaded[name], pltpu.HBM) for name in LOADED]
    held_slots = n_cells * slots if n_cells <= 16 else LANES
    wind_out, spectra_out = pl.pallas_call(
        functools.partial(kernel, n_cells, n_spec),
        out_shape=(
            jax.ShapeDtypeStruct(wind_field.shape, f32),
            jax.ShapeDtypeStruct((bands, DIRECTIONS, ocean), f32),
        ),
        in_specs=[hbm] * len(loaded),
        out_specs=(vmem, vmem),
        scratch_shapes=[
            *(pltpu.VMEM(array.shape, array.dtype) for array in loaded[:-2]),
            *(pltpu.SMEM(array.shape, array.dtype) for array in loaded[-2:]),
            pltpu.VMEM((2 * levels, cells + 2 * rim), f32),
            pltpu.VMEM((2 * levels, cells + 2 * rim), f32),
            pltpu.VMEM((2, 2 * levels, rim), f32),
            pltpu.VMEM((2, 2 * levels, rim), f32),
            pltpu.VMEM((2, cells), f32),
            pltpu.VMEM((n_cells + 2, 2, slots), f32),
            pltpu.VMEM((n_cells, 3, 2, slots), f32),
            pltpu.VMEM((ocean, held_slots), jnp.bfloat16),
            pltpu.VMEM((2, LANES, held_slots), jnp.bfloat16),
            pltpu.VMEM((2, n_cells, slots), jnp.int32),
            pltpu.VMEM((2, 2, LANES), jnp.int32),
            pltpu.VMEM((2, ocean), f32),
            pltpu.VMEM((n_spec, 2, ocean), f32),
            pltpu.VMEM((2, ROWS, LANES), f32),
            pltpu.VMEM((2, 3, ocean), f32),
            pltpu.VMEM((2, bands * ROWS, LANES), f32),
            pltpu.VMEM((bands * ROWS, ocean + 2 * LANES), f32),
            dma((len(loaded),)), dma((4,)), dma((4,)), dma((n_spec,)), dma((n_spec,)), dma((n_spec,)), dma,
            dma((n_cells,)), dma((n_cells,)), dma((2,)), dma((2,)), dma((4,)), dma((4,)),
        ],
        compiler_params=pltpu.CompilerParams(
            collective_id=0, has_side_effects=True, vmem_limit_bytes=32 * 2**20
        ),
    )(*loaded)
    return wind_out, jnp.transpose(spectra_out, (1, 0, 2))


def solution(mesh):
    in_specs = (
        P(None, "spec", "cells"),
        P("spec"),
        P(None, "cells"),
        P(None, "cells"),
        P("cells"),
        P("cells", None),
        P("cells"),
        P("cells", None),
        P("cells", None),
        P(None, "spec", "cells"),
        P("cells"),
        P(None, "cells"),
        P(None, "cells"),
        P(None, "cells"),
        P("cells"),
    )
    out_specs = (P(None, "spec", "cells"), P(None, "spec", "cells"))
    body = functools.partial(local, mesh.shape["cells"], mesh.shape["spec"])
    return jax.shard_map(body, mesh=mesh, in_specs=in_specs, out_specs=out_specs, check_vma=False)
```

```python
import functools
import math

import jax
import jax.numpy as jnp
from jax import lax
from jax.experimental import pallas as pl
from jax.experimental.pallas import tpu as pltpu
from jax.sharding import PartitionSpec as P

DIRECTIONS = 36
BANDS = 12
ROWS = 40
LANES = 128
MESH = pl.DeviceIdType.MESH
LOADED = (
    "wind", "atm_send", "spectra", "sea_mask", "atm_table", "atm_coef", "recv_cells", "ocn_send", "face_angle",
    "face_ratio", "slot_weight", "send_cells", "ocn_table", "damping", "block_count",
)

epsilon = 1e-06
wind_factor = 0.8
growth = 0.1
coupling = 4.0
dissipation = 0.05


def lane_take(tile, lane):
    return jnp.take_along_axis(tile, lane, axis=1, mode="promise_in_bounds")


def pick(tiles, lane, high, first):
    found = lane_take(tiles[0], lane)
    for j in range(1, len(tiles)):
        found = jnp.where(high == first + j, lane_take(tiles[j], lane), found)
    return found


def spread8(row):
    return jnp.broadcast_to(row, (8, row.shape[1]))


def split_index(index):
    return lax.bitwise_and(index, LANES - 1), lax.shift_right_logical(index, 7)


def kernel(
    n_cells, n_spec,
    *refs,
):
    count = len(LOADED)
    given, (wind_out, spectra_out), held = refs[:count], refs[count:count + 2], refs[count + 2:2 * count + 2]
    (wind, atm_send, spectra, sea_mask, atm_table, atm_coef, recv_cells, ocn_send, face_angle, face_ratio, slot_weight,
     send_cells, ocn_table, damping, block_count) = held
    (ext0, names, weights, name_rim, weight_rim, name_got, weight_got, far, more_ssem, more_rsem,
     ext1, ext2, rim1, rim2, surf, blk_send, blk_recv, onehot, onehot_rim, near_recv, near_send, means_own, means,
     trig, faces, ocn_rim, ocn_ext,
     load_sem, atm_ssem, atm_rsem, mean_ssem, mean_rsem, surf_ssem, surf_rsem, blk_ssem, blk_rsem, ocn_ssem, ocn_rsem,
     near_ssem, near_rsem) = refs[2 * count + 2:]
    me = lax.axis_index("cells")
    part = lax.axis_index("spec")
    before, after = lax.rem(me + n_cells - 1, n_cells), lax.rem(me + 1, n_cells)
    levels, cells = wind.shape[1], wind.shape[2]
    own_tiles = cells // LANES
    rim = rim1.shape[2]
    rim_tiles = rim // LANES
    bands, ocean = spectra.shape[0], spectra.shape[2]
    ocean_tiles = ocean // LANES
    slots = send_cells.shape[1]
    stored = n_cells <= 16

    barrier = pltpu.get_barrier_semaphore()

    def greet_cells(step, carry):
        other = lax.rem(me + step, n_cells)
        pl.semaphore_signal(barrier, inc=1, device_id=(other, part), device_id_type=MESH)
        return carry

    def greet_spec(step, carry):
        other = lax.rem(part + step, n_spec)
        pl.semaphore_signal(barrier, inc=1, device_id=(me, other), device_id_type=MESH)
        return carry

    lax.fori_loop(1, n_cells, greet_cells, 0)
    lax.fori_loop(1, n_spec, greet_spec, 0)

    loads = [pltpu.make_async_copy(given[q], held[q], load_sem.at[q]) for q in range(count)]
    for load in loads:
        load.start()

    def gather_rim(ext, out, base=None):
        base = rim if base is None else base
        tiles = [ext[:, pl.ds(base + j * LANES, LANES)] for j in range(own_tiles)]
        for t in range(2 * rim_tiles):
            lane, high = split_index(spread8(atm_send[pl.ds(t, 1), :]))
            out[t // rim_tiles, :, pl.ds((t % rim_tiles) * LANES, LANES)] = pick(tiles, lane, high, 0)

    def rim_copies(out, ext, base):
        to_before = pltpu.make_async_remote_copy(
            src_ref=out.at[0], dst_ref=ext.at[:, pl.ds(rim + cells, rim)],
            send_sem=atm_ssem.at[base], recv_sem=atm_rsem.at[base],
            device_id=(before, part), device_id_type=MESH)
        to_after = pltpu.make_async_remote_copy(
            src_ref=out.at[1], dst_ref=ext.at[:, pl.ds(0, rim)],
            send_sem=atm_ssem.at[base + 1], recv_sem=atm_rsem.at[base + 1],
            device_id=(after, part), device_id_type=MESH)
        return to_before, to_after

    def laplace(ext, store):
        def block(b, carry):
            start = pl.multiple_of(b * LANES, LANES)
            here = ext[:, pl.ds(rim + start, LANES)]
            tiles = [ext[:, pl.ds(start + j * LANES, LANES)] for j in range(2 * rim_tiles + 1)]
            total = jnp.zeros((8, LANES), jnp.float32)
            for k in range(3):
                lane, high = split_index(spread8(atm_table[pl.ds(k, 1), pl.ds(start, LANES)]))
                near = pick(tiles, lane, high - b, 0)
                total += spread8(atm_coef[pl.ds(k, 1), pl.ds(start, LANES)]) * (near - here)
            store(start, here, total)
            return carry

        lax.fori_loop(0, own_tiles, block, 0, unroll=4)

    for load in loads:
        load.wait()
    ext1[0:levels, pl.ds(rim, cells)] = wind[0]
    ext1[levels:2 * levels, pl.ds(rim, cells)] = wind[1]
    gather_rim(ext1, rim1)
    for side in (0, rim + cells):
        ext0[:, pl.ds(side, rim)] = jnp.zeros((2 * levels, rim), jnp.float32)
    ext0[0:levels, pl.ds(rim, cells)] = wind[0]
    ext0[levels:2 * levels, pl.ds(rim, cells)] = wind[1]

    def keep_once(start, here, lap):
        ext2[:, pl.ds(rim + start, LANES)] = lap

    laplace(ext0, keep_once)
    gather_rim(ext2, rim2)
    names[...] = jnp.zeros_like(names)
    weights[...] = jnp.zeros_like(weights)
    names[0:3, :] = atm_table[...]
    weights[0:3, :] = atm_coef[...]
    gather_rim(names, name_rim, 0)
    gather_rim(weights, weight_rim, 0)
    pl.semaphore_wait(barrier, n_cells + n_spec - 2)
    first = rim_copies(rim1, ext1, 0)
    for copy in first:
        copy.start()
    second = rim_copies(rim2, ext2, 2)
    more = []
    for side, step in ((0, n_cells - 1), (1, 1)):
        moves = ((name_rim, name_got, step), (weight_rim, weight_got, step), (rim1, far, 2 * step))
        for q, (src, dst, by) in enumerate(moves):
            more.append(pltpu.make_async_remote_copy(
                src_ref=src.at[side], dst_ref=dst.at[1 - side],
                send_sem=more_ssem.at[3 * side + q], recv_sem=more_rsem.at[3 * side + q],
                device_id=(lax.rem(me + by, n_cells), part), device_id_type=MESH))
    for copy in (*second, *more):
        copy.start()

    def near_copies(side, other):
        at = 1 - side
        return [
            pltpu.make_async_remote_copy(
                src_ref=src, dst_ref=dst.at[at], send_sem=near_ssem.at[2 * at + q], recv_sem=near_rsem.at[2 * at + q],
                device_id=(other, part), device_id_type=MESH)
            for q, (src, dst) in enumerate(((recv_cells, near_recv), (ocn_send, near_send)))
        ]

    near = near_copies(0, before) + near_copies(1, after)
    for copy in near:
        copy.start()

    mask = sea_mask[...].astype(jnp.float32)
    frequency = []
    for k in range(bands):
        value = jnp.float32(0.6 * 1.1**k)
        for s in range(1, n_spec):
            value = jnp.where(part == s, jnp.float32(0.6 * 1.1 ** (s * bands + k)), value)
        frequency.append(value)
    total = jnp.zeros((1, ocean), jnp.float32)
    inverse = jnp.zeros((1, ocean), jnp.float32)
    for k in range(bands):
        band_sum = jnp.sum(spectra[k] * mask, axis=0, keepdims=True)
        total += band_sum
        inverse += band_sum * (1.0 / jnp.full((1, ocean), frequency[k], jnp.float32))
    means_own[0:1, :] = total
    means_own[1:2, :] = inverse

    def mean_copy(other, slot):
        return pltpu.make_async_remote_copy(
            src_ref=means_own, dst_ref=means.at[slot],
            send_sem=mean_ssem.at[other], recv_sem=mean_rsem.at[slot],
            device_id=(me, other), device_id_type=MESH)

    for step in range(1, n_spec):
        mean_copy(lax.rem(part + step, n_spec), part).start()

    for copy in first:
        copy.wait_recv()

    laplace(ext1, keep_once)

    def hits(i):
        place = lax.broadcasted_iota(jnp.int32, (ocean, slots), 0)
        return jnp.where(place == recv_cells[pl.ds(i, 1), :], 1.0, 0.0).astype(jnp.bfloat16)

    def rim_hits(side, column, i):
        return jnp.where(column == near_recv[side, pl.ds(i, 1), :], 1.0, 0.0).astype(jnp.bfloat16)

    for copy in near:
        copy.wait_recv()
    columns = []
    for side in range(2):
        names = near_send[side, 1 - side:2 - side, :].astype(jnp.float32)
        column = jnp.transpose(jnp.broadcast_to(names, (LANES, LANES))).astype(jnp.int32)
        columns.append(jnp.concatenate([column] * (slots // LANES), axis=1))
    if stored:
        for i in range(n_cells):
            at = slice(i * slots, (i + 1) * slots)
            onehot[:, at] = hits(i)
            for side in range(2):
                onehot_rim[side, :, at] = rim_hits(side, columns[side], i)
    heading = (lax.broadcasted_iota(jnp.int32, (ROWS, LANES), 0).astype(jnp.float32) + 0.5) * (
        2.0 * math.pi / DIRECTIONS
    )
    trig[0] = jnp.cos(heading)
    trig[1] = jnp.sin(heading)
    angle = face_angle[...]
    ratio = face_ratio[...]
    faces[0] = jnp.cos(angle) * ratio
    faces[1] = jnp.sin(angle) * ratio
    total = means_own[0:1, :]
    inverse = means_own[1:2, :]
    for step in range(1, n_spec):
        other = lax.rem(part + step, n_spec)
        mean_copy(other, other).wait_recv()
        total += means[other, 0:1, :]
        inverse += means[other, 1:2, :]
    components = DIRECTIONS * BANDS
    mean_energy = total / components
    mean_freq = mean_energy / (inverse / components + epsilon)
    squared = mean_freq * mean_freq
    for k in range(bands):
        decay = (dissipation * frequency[k]) * (mean_energy * (squared * squared))
        own = pl.ds(LANES, ocean)
        ocn_ext[k * ROWS + 32:(k + 1) * ROWS, own] = jnp.zeros((8, ocean), jnp.float32)
        ocn_ext[k * ROWS:k * ROWS + DIRECTIONS, own] = spectra[k] * (mask * (1.0 / (1.0 + decay)))
    for side in range(2):
        lane, high = split_index(spread8(ocn_send[side:side + 1, :]))
        for r in range(bands * ROWS // 8):
            rows = slice(r * 8, r * 8 + 8)
            tiles = [ocn_ext[rows, LANES + j * LANES:LANES + (j + 1) * LANES] for j in range(ocean_tiles)]
            ocn_rim[side, rows, :] = pick(tiles, lane, high, 0)
    third = (
        pltpu.make_async_remote_copy(
            src_ref=ocn_rim.at[0], dst_ref=ocn_ext.at[:, pl.ds(ocean + LANES, LANES)],
            send_sem=ocn_ssem.at[0], recv_sem=ocn_rsem.at[0],
            device_id=(before, part), device_id_type=MESH),
        pltpu.make_async_remote_copy(
            src_ref=ocn_rim.at[1], dst_ref=ocn_ext.at[:, pl.ds(0, LANES)],
            send_sem=ocn_ssem.at[1], recv_sem=ocn_rsem.at[1],
            device_id=(after, part), device_id_type=MESH),
    )
    for copy in third:
        copy.start()

    for copy in (*second, *more):
        copy.wait_recv()
    for side in range(2):
        sources = (far, rim1) if side == 0 else (rim1, far)
        for t in range(rim_tiles):
            at = pl.ds(t * LANES, LANES)
            spot = pl.ds(side * (rim + cells) + t * LANES, LANES)
            total = ext2[:, spot]
            for k in range(3):
                lane, high = split_index(spread8(name_got[side, k:k + 1, at]))
                low, top = (
                    pick([source[q, :, pl.ds(j * LANES, LANES)] for j in range(rim_tiles)], lane, high, first_tile)
                    for q, (source, first_tile) in enumerate(
                        zip(sources, (0, rim_tiles + own_tiles)))
                    for q in [side]
                )
                value = jnp.where(high < rim_tiles, low, jnp.where(high >= rim_tiles + own_tiles, top, 0.0))
                total += spread8(weight_got[side, k:k + 1, at]) * value
            ext2[:, spot] = total
    row = lax.broadcasted_iota(jnp.int32, (8, LANES), 0)
    rate = jnp.zeros((8, LANES), jnp.float32)
    for v in range(levels):
        rate = jnp.where(lax.rem(row, levels) == v, damping[v], rate)

    def keep_damped(start, here, lap):
        damped = ext1[:, pl.ds(rim + start, LANES)] - rate * lap
        wind_out[0, :, pl.ds(start, LANES)] = damped[0:levels]
        wind_out[1, :, pl.ds(start, LANES)] = damped[levels:2 * levels]

    laplace(ext2, keep_damped)

    def surf_copy(other):
        return pltpu.make_async_remote_copy(
            src_ref=surf, dst_ref=surf, send_sem=surf_ssem.at[other], recv_sem=surf_rsem,
            device_id=(me, other), device_id_type=MESH)

    @pl.when(part == n_spec - 1)
    def _():
        surf[0:1, :] = wind_factor * wind_out[0, levels - 1:levels, :]
        surf[1:2, :] = wind_factor * wind_out[1, levels - 1:levels, :]
        for other in range(n_spec - 1):
            surf_copy(other).start()

    @pl.when(part != n_spec - 1)
    def _():
        surf_copy(0).wait_recv()

    for g in range(n_cells // 8):
        row = lax.broadcasted_iota(jnp.int32, (8, LANES), 0)
        live = jnp.zeros((8, LANES), jnp.int32)
        for i in range(8):
            live = jnp.where(row == i, block_count[g * 8 + i], live)
        for h in range(slots // LANES):
            spot = lax.broadcasted_iota(jnp.int32, (8, LANES), 1) + h * LANES
            scale = jnp.where(spot < live, slot_weight[g * 8:g * 8 + 8, pl.ds(h * LANES, LANES)], 0.0)
            lane, high = split_index(send_cells[g * 8:g * 8 + 8, pl.ds(h * LANES, LANES)])
            for c in range(2):
                tiles = [spread8(surf[c:c + 1, pl.ds(j * LANES, LANES)]) for j in range(own_tiles)]
                blk_send[g * 8 + 1:g * 8 + 9, c, pl.ds(h * LANES, LANES)] = scale * pick(tiles, lane, high, 0)

    blk_send[0] = blk_send[n_cells]
    blk_send[n_cells + 1] = blk_send[1]

    def block_copy(other, slot):
        return pltpu.make_async_remote_copy(
            src_ref=blk_send.at[pl.ds(other, 3)], dst_ref=blk_recv.at[slot],
            send_sem=blk_ssem.at[other], recv_sem=blk_rsem.at[slot],
            device_id=(other, part), device_id_type=MESH)

    def send_block(step, carry):
        block_copy(lax.rem(me + step, n_cells), me).start()
        return carry

    lax.fori_loop(1, n_cells, send_block, 0)
    for r in range(3):
        blk_recv[me, r] = blk_send[me + r]

    def wait_block(step, carry):
        other = lax.rem(me + step, n_cells)
        block_copy(other, other).wait_recv()
        return carry

    lax.fori_loop(1, n_cells, wait_block, 0)

    def product(value, ones):
        high = value.astype(jnp.bfloat16).astype(jnp.float32)
        rest = value - high
        middle = rest.astype(jnp.bfloat16).astype(jnp.float32)
        parts = jnp.concatenate([high, middle, rest - middle, jnp.zeros_like(high)], axis=0)
        return lax.dot_general(
            parts.astype(jnp.bfloat16), ones, (((1,), (1,)), ((), ())), preferred_element_type=jnp.float32)

    def deposit(i, sums):
        if stored:
            at = slice(i * slots, (i + 1) * slots)
            ones = [onehot_rim[0, :, at], onehot[:, at], onehot_rim[1, :, at]]
        else:
            ones = [rim_hits(0, columns[0], i), hits(i), rim_hits(1, columns[1], i)]
        return tuple(acc + product(blk_recv[i, r], ones[r]) for r, acc in enumerate(sums))

    sums = tuple(jnp.zeros((8, width), jnp.float32) for width in (LANES, ocean, LANES))
    if stored:
        for i in range(n_cells):
            sums = deposit(i, sums)
    else:
        sums = lax.fori_loop(0, n_cells, deposit, sums)
    acc = jnp.concatenate(sums, axis=1)
    wind_u = acc[0:1] + acc[2:3] + acc[4:5]
    wind_v = acc[1:2] + acc[3:4] + acc[5:6]

    for copy in third:
        copy.wait_recv()
    for g in range(ROWS // 8):
        rows = slice(g * 8, g * 8 + 8)
        for b in range(ocean_tiles + 2):
            at = slice(b * LANES, (b + 1) * LANES)
            along = trig[0, rows, :] * wind_u[:, at] + trig[1, rows, :] * wind_v[:, at]
            for k in range(bands):
                gain = (growth * frequency[k]) * jnp.maximum((coupling * frequency[k]) * along - 1.0, 0.0)
                spot = slice(k * ROWS + g * 8, k * ROWS + g * 8 + 8)
                ocn_ext[spot, at] = ocn_ext[spot, at] * (1.0 + gain)

    for b in range(ocean_tiles):
        at = slice(b * LANES, (b + 1) * LANES)
        index = [split_index(spread8(ocn_table[f:f + 1, at])) for f in range(3)]
        for g in range(ROWS // 8):
            normal = [
                trig[0, g * 8:g * 8 + 8, :] * faces[0, f:f + 1, at] + trig[1, g * 8:g * 8 + 8, :] * faces[1, f:f + 1, at]
                for f in range(3)
            ]
            for k in range(bands):
                speed = 0.5 / jnp.full((8, LANES), frequency[k], jnp.float32)
                rows = slice(k * ROWS + g * 8, k * ROWS + g * 8 + 8)
                tiles = [ocn_ext[rows, (b + j) * LANES:(b + j + 1) * LANES] for j in range(3)]
                here = tiles[1]
                result = here
                for f in range(3):
                    transport = speed * normal[f]
                    upwind = pick(tiles, index[f][0], index[f][1], b)
                    result = result - transport * jnp.where(transport > 0.0, here, upwind)
                size = min(8, DIRECTIONS - g * 8)
                spectra_out[k, g * 8:g * 8 + size, at] = result[0:size]
    for copy in (*first, *second, *third, *near, *more):
        copy.wait_send()
    for step in range(1, n_spec):
        mean_copy(lax.rem(part + step, n_spec), part).wait_send()

    @pl.when(part == n_spec - 1)
    def _():
        for other in range(n_spec - 1):
            surf_copy(other).wait_send()

    def sent_block(step, carry):
        block_copy(lax.rem(me + step, n_cells), me).wait_send()
        return carry

    lax.fori_loop(1, n_cells, sent_block, 0)


def local(
    n_cells, n_spec,
    wind_field, damping, atm_table, atm_coef, atm_send, send_cells, block_count, slot_weight, recv_cells,
    spectra, sea_mask, ocn_table, face_angle, face_ratio, ocn_send,
):
    levels, cells = wind_field.shape[1:]
    rim = atm_send.shape[0] // 2
    bands, ocean = spectra.shape[1:]
    slots = send_cells.shape[1]
    f32 = jnp.float32
    vmem = pl.BlockSpec(memory_space=pltpu.VMEM)
    hbm = pl.BlockSpec(memory_space=pltpu.HBM)
    dma = pltpu.SemaphoreType.DMA
    loaded = dict(
        wind=wind_field, atm_send=atm_send.reshape(-1, LANES), spectra=jnp.transpose(spectra, (1, 0, 2)),
        sea_mask=sea_mask.reshape(1, -1), atm_table=atm_table, atm_coef=atm_coef, recv_cells=recv_cells,
        ocn_send=ocn_send.reshape(-1, LANES), face_angle=face_angle, face_ratio=face_ratio, slot_weight=slot_weight,
        send_cells=send_cells, ocn_table=ocn_table, damping=damping, block_count=block_count,
    )
    loaded = [pltpu.with_memory_space_constraint(loaded[name], pltpu.HBM) for name in LOADED]
    held_slots = n_cells * slots if n_cells <= 16 else LANES
    wind_out, spectra_out = pl.pallas_call(
        functools.partial(kernel, n_cells, n_spec),
        out_shape=(
            jax.ShapeDtypeStruct(wind_field.shape, f32),
            jax.ShapeDtypeStruct((bands, DIRECTIONS, ocean), f32),
        ),
        in_specs=[hbm] * len(loaded),
        out_specs=(vmem, vmem),
        scratch_shapes=[
            *(pltpu.VMEM(array.shape, array.dtype) for array in loaded[:-2]),
            *(pltpu.SMEM(array.shape, array.dtype) for array in loaded[-2:]),
            pltpu.VMEM((2 * levels, cells + 2 * rim), f32),
            pltpu.VMEM((8, cells), jnp.int32), pltpu.VMEM((8, cells), f32),
            pltpu.VMEM((2, 8, rim), jnp.int32), pltpu.VMEM((2, 8, rim), f32),
            pltpu.VMEM((2, 8, rim), jnp.int32), pltpu.VMEM((2, 8, rim), f32),
            pltpu.VMEM((2, 2 * levels, rim), f32), dma((6,)), dma((6,)),
            pltpu.VMEM((2 * levels, cells + 2 * rim), f32),
            pltpu.VMEM((2 * levels, cells + 2 * rim), f32),
            pltpu.VMEM((2, 2 * levels, rim), f32),
            pltpu.VMEM((2, 2 * levels, rim), f32),
            pltpu.VMEM((2, cells), f32),
            pltpu.VMEM((n_cells + 2, 2, slots), f32),
            pltpu.VMEM((n_cells, 3, 2, slots), f32),
            pltpu.VMEM((ocean, held_slots), jnp.bfloat16),
            pltpu.VMEM((2, LANES, held_slots), jnp.bfloat16),
            pltpu.VMEM((2, n_cells, slots), jnp.int32),
            pltpu.VMEM((2, 2, LANES), jnp.int32),
            pltpu.VMEM((2, ocean), f32),
            pltpu.VMEM((n_spec, 2, ocean), f32),
            pltpu.VMEM((2, ROWS, LANES), f32),
            pltpu.VMEM((2, 3, ocean), f32),
            pltpu.VMEM((2, bands * ROWS, LANES), f32),
            pltpu.VMEM((bands * ROWS, ocean + 2 * LANES), f32),
            dma((len(loaded),)), dma((4,)), dma((4,)), dma((n_spec,)), dma((n_spec,)), dma((n_spec,)), dma,
            dma((n_cells,)), dma((n_cells,)), dma((2,)), dma((2,)), dma((4,)), dma((4,)),
        ],
        compiler_params=pltpu.CompilerParams(
            collective_id=0, has_side_effects=True, vmem_limit_bytes=32 * 2**20
        ),
    )(*loaded)
    return wind_out, jnp.transpose(spectra_out, (1, 0, 2))


def solution(mesh):
    in_specs = (
        P(None, "spec", "cells"),
        P("spec"),
        P(None, "cells"),
        P(None, "cells"),
        P("cells"),
        P("cells", None),
        P("cells"),
        P("cells", None),
        P("cells", None),
        P(None, "spec", "cells"),
        P("cells"),
        P(None, "cells"),
        P(None, "cells"),
        P(None, "cells"),
        P("cells"),
    )
    out_specs = (P(None, "spec", "cells"), P(None, "spec", "cells"))
    body = functools.partial(local, mesh.shape["cells"], mesh.shape["spec"])
    return jax.shard_map(body, mesh=mesh, in_specs=in_specs, out_specs=out_specs, check_vma=False)
```
